32 devices in a mesh: parts: 2 (over y), tp: 4 (over z), page: 2 (over x), sub: 2 (over core).
Axes of the slice: x: 2, y: 2, z: 4, core: 2. Of those that a mesh axis runs over, the one named last changes fastest.
Arguments:
- hidden_units: bfloat16 [128, 33792], P('parts', 'tp'), parts along dimension 0, may hold values from -6 to 6
- adapter_ids: int32 [128], P('parts'), parts along dimension 0, may hold values from 0 to 3
- down_projection_weight: bfloat16 [33792, 12288], P('tp', ('page', 'sub')), may hold values from -0.03125 to 0.03125
- rank_down: bfloat16 [8, 33792, 64], P(('parts', 'page', 'sub'), 'tp'), parts along dimension 0, may hold values from -0.03125 to 0.03125
- rank_up: bfloat16 [8, 64, 12288], P(('parts', 'tp'), None, ('page', 'sub')), parts along dimension 0, may hold values from -0.75 to 0.75
- residual: bfloat16 [128, 12288], P(('parts', 'tp'), ('page', 'sub')), parts along dimension 0, may hold values from -6 to 6
Outputs:
- mixed: bfloat16 [128, 12288], P(('parts', 'tp'), ('page', 'sub')), parts along dimension 0
The draws below stay inside these ranges and needn't reach their ends.
There are 2 independent parts, one for each index of `parts`. The reference program is written for one: setup_inputs(seed, part) draws one part's arguments, and reference() takes and returns one part's arrays. A program takes and returns all parts, laid end to end along the dimension named above; an argument that names none is the same for every part. Nothing has to cross between parts.
All inputs are finite; a program needn't handle non-finite values.
Results may differ from the reference program's by a relative error of at most 0.0095.
Values may be sent and summed in bfloat16 or wider, within the bound.
No kernel may reach another device: no remote copies, remote signals or barrier semaphores. Data moves between devices by JAX's collectives and lax.ppermute only.
A program may use at most 128 MiB of HBM per device.

```python
import math
import jax
import jax.numpy as jnp
import numpy as np
from jax import lax

D = 12288
FF = 33792
R = 64
ROWS = 64
ADAPTERS = 4
N_TP = 4


def with_ends(result, stream_key, low, largest):
    index_at = [jax.random.randint(jax.random.fold_in(stream_key, axis), (), 0, length) for axis, length in enumerate(result.shape)]
    widest = result.shape.index(max(result.shape))
    neighbour = index_at[:widest] + [(index_at[widest] + 1) % result.shape[widest]] + index_at[widest + 1:]
    return result.at[tuple(index_at)].set(low).at[tuple(neighbour)].set(largest)


def level_of(rng, extent, cuts, least, largest):
    loudness = 1.0
    for dim, shards_of in cuts:
        steps = jax.random.uniform(jax.random.fold_in(jax.random.fold_in(rng, 6), dim), (shards_of,), jnp.float32, least / len(cuts), largest / len(cuts))
        loudness = loudness * jnp.repeat(jnp.exp(steps), extent[dim] // shards_of).reshape((-1,) + (1,) * (len(extent) - 1 - dim))
    return loudness


def rank_table(number_of, slope):
    loads = [(1 << 20) // math.isqrt(standing ** slope) + 1 for standing in range(1, number_of + 1)]
    width = 1 + sum(loads) // (1 << 30)
    return np.cumsum(np.array([max(1, weight // width) for weight in loads]))


def ranked_ids(stream_key, extent, count, slope):
    table = rank_table(count, slope)
    pick = jax.random.randint(jax.random.fold_in(stream_key, 1), extent, 0, int(table[count - 1]))
    rank = jnp.searchsorted(jnp.asarray(table, jnp.int32), pick, side="right")
    return jax.random.permutation(jax.random.fold_in(stream_key, 2), count)[rank].astype(jnp.int32)


def gaussian(own_key, extent, spread, bound, pieces=(), kind=jnp.bfloat16):
    factor_of = level_of(own_key, extent, pieces, -0.22, 0.18) if pieces else 1.0
    values = jax.random.normal(own_key, extent, jnp.float32) * spread * factor_of
    return jnp.minimum(jnp.maximum(values, -bound), bound).astype(kind)


def setup_inputs(seed: int = 0, part: int = 0) -> dict:
    arg_keys = jax.random.split(jax.random.key(seed), 7)
    own_keys = jax.random.split(jax.random.fold_in(arg_keys[6], part), 7)
    return {
        "hidden_units": gaussian(own_keys[0], (ROWS, FF), 1.0, 6.0, ((1, 4),)),
        "adapter_ids": with_ends(ranked_ids(own_keys[1], (ROWS,), ADAPTERS, 2), jax.random.fold_in(own_keys[1], 3), 0, ADAPTERS - 1).astype(jnp.int32),
        "down_projection_weight": gaussian(arg_keys[2], (FF, D), FF ** -0.5, 0.03125, ((0, 4), (1, 4))),
        "rank_down": gaussian(own_keys[3], (ADAPTERS, FF, R), FF ** -0.5, 0.03125, ((0, 4), (1, 4))),
        "rank_up": gaussian(own_keys[4], (ADAPTERS, R, D), R ** -0.5, 0.75, ((0, 4), (2, 4))),
        "residual": gaussian(own_keys[5], (ROWS, D), 1.0, 6.0, ((0, 4), (1, 4))),
    }


def reference(hidden_units, adapter_ids, down_projection_weight, rank_down, rank_up, residual):
    chosen = (adapter_ids[:, None] == jnp.arange(ADAPTERS, dtype=jnp.int32)[None, :]).astype(jnp.float32)
    flattened = jnp.transpose(rank_down, (1, 0, 2)).reshape(FF, ADAPTERS * R)
    projected = jnp.dot(hidden_units, flattened, preferred_element_type=jnp.float32).reshape(ROWS, ADAPTERS, R)
    low_rank = jnp.einsum("rak,ra->rk", projected, chosen).astype(jnp.bfloat16)
    block_width = FF // N_TP
    block_adapters = ADAPTERS // N_TP

    def addend_block_part(total, index):
        start = (index * block_width).astype(jnp.int32)
        hidden_block = lax.dynamic_slice_in_dim(hidden_units, start, block_width, 1)
        weight_block = lax.dynamic_slice_in_dim(down_projection_weight, start, block_width, 0)
        base_projection_term = jnp.dot(hidden_block, weight_block, preferred_element_type=jnp.float32)
        first = (index * block_adapters).astype(jnp.int32)
        picked = ((adapter_ids - first)[:, None] == jnp.arange(block_adapters, dtype=jnp.int32)[None, :]).astype(jnp.float32)
        low_rank_coefficient = (picked[:, :, None] * low_rank.astype(jnp.float32)[:, None, :]).reshape(ROWS, block_adapters * R).astype(jnp.bfloat16)
        up_weight_block = lax.dynamic_slice_in_dim(rank_up, first, block_adapters, 0).reshape(block_adapters * R, D)
        adapter_correction_term = jnp.dot(low_rank_coefficient, up_weight_block, preferred_element_type=jnp.float32)
        rounded_result = lax.optimization_barrier((base_projection_term + adapter_correction_term).astype(jnp.bfloat16))
        return total + rounded_result.astype(jnp.float32), None

    start_total = residual.astype(jnp.float32)
    total, unused = lax.scan(addend_block_part, start_total, jnp.arange(N_TP, dtype=jnp.int32))
    return total.astype(jnp.bfloat16)
```

```python
import jax
import jax.numpy as jnp
from jax import lax
from jax.sharding import PartitionSpec as P

CHUNKS = 3


def gathered_low_rank(partial_low):
    n_tp, n_page, n_sub = (lax.axis_size(axis) for axis in ("tp", "page", "sub"))
    n_ps = n_page * n_sub
    if n_tp != n_ps:
        return lax.psum(partial_low, ("tp", "page", "sub")).astype(jnp.bfloat16)
    total = None
    for j in range(n_tp):
        pairs = [
            (t * n_ps + a, a * n_ps + (t + j) % n_tp) for t in range(n_tp) for a in range(n_ps)
        ]
        got = lax.ppermute(partial_low, ("tp", "page", "sub"), pairs)
        total = got if total is None else total + got
    return total.astype(jnp.bfloat16)


def on_device(hidden_units, adapter_ids, down_projection_weight, rank_down, rank_up, residual):
    n_tp = lax.axis_size("tp")
    tp = lax.axis_index("tp")
    owned_count = rank_down.shape[0]
    first_owned = lax.axis_index(("page", "sub")) * owned_count
    chosen = (
        (adapter_ids - first_owned)[:, None] == jnp.arange(owned_count, dtype=jnp.int32)[None, :]
    ).astype(jnp.float32)
    projected = jnp.einsum(
        "rf,afk->rak", hidden_units, rank_down, preferred_element_type=jnp.float32
    )
    partial_low = jnp.einsum("rak,ra->rk", projected, chosen)
    low_rank = gathered_low_rank(partial_low)
    held_count, rank_width, columns = rank_up.shape
    first_held = tp * held_count
    flattened = rank_up.reshape(held_count * rank_width, columns)
    rows_dev = residual.shape[0]
    picked = (
        (adapter_ids - first_held)[:, None] == jnp.arange(held_count, dtype=jnp.int32)[None, :]
    ).astype(jnp.bfloat16)
    coefficient = (picked[:, :, None] * low_rank[:, None, :]).reshape(
        n_tp * rows_dev, held_count * rank_width
    )
    width = columns // CHUNKS
    pieces = []
    for c in range(CHUNKS):
        at = slice(c * width, (c + 1) * width)
        base = jnp.dot(
            hidden_units, down_projection_weight[:, at], preferred_element_type=jnp.float32
        )
        term = (
            base + jnp.dot(coefficient, flattened[:, at], preferred_element_type=jnp.float32)
        ).astype(jnp.bfloat16)
        if n_tp > 4:
            summed = lax.psum_scatter(
                term, "tp", scatter_dimension=0, tiled=True
            ).astype(jnp.float32)
        else:
            block = lambda to: lax.dynamic_slice_in_dim(term, to * rows_dev, rows_dev, 0)
            summed = block(tp).astype(jnp.float32)
            for shift in range(1, n_tp):
                got = lax.ppermute(
                    block((tp + shift) % n_tp), "tp", [(i, (i + shift) % n_tp) for i in range(n_tp)]
                )
                summed = summed + got.astype(jnp.float32)
        pieces.append((residual[:, at].astype(jnp.float32) + summed).astype(jnp.bfloat16))
    return jnp.concatenate(pieces, axis=1)


def solution(mesh):
    placed = (
        P("parts", "tp"),
        P("parts"),
        P("tp", ("page", "sub")),
        P(("parts", "page", "sub"), "tp", None),
        P(("parts", "tp"), None, ("page", "sub")),
        P(("parts", "tp"), ("page", "sub")),
    )
    return jax.shard_map(
        on_device,
        mesh=mesh,
        in_specs=placed,
        out_specs=P(("parts", "tp"), ("page", "sub")),
        check_vma=False,
    )
```

```python
import functools

import jax
import jax.numpy as jnp
from jax import lax
from jax.experimental import pallas as pl
from jax.experimental.pallas import tpu as pltpu
from jax.sharding import PartitionSpec as P

CHUNKS = (1024, 1024, 1024)
PS = ("page", "sub")


def low_kernel(hidden, rank_down, chosen, out):
    total = jnp.zeros(out.shape, jnp.float32)
    for a in range(rank_down.shape[0]):
        product = lax.dot_general(
            hidden[...], rank_down[a], (((1,), (1,)), ((), ())), preferred_element_type=jnp.float32
        )
        total = total + product * chosen[:, a : a + 1]
    out[...] = total


def partial_low_rank(hidden_units, rank_down, chosen):
    rows = hidden_units.shape[0]
    rank = rank_down.shape[2]
    return pl.pallas_call(
        low_kernel,
        out_shape=jax.ShapeDtypeStruct((rows, rank), jnp.float32),
        in_specs=[pl.BlockSpec(memory_space=pltpu.VMEM)] * 3,
        out_specs=pl.BlockSpec(memory_space=pltpu.VMEM),
        compiler_params=pltpu.CompilerParams(vmem_limit_bytes=16 << 20),
        name="low_rank",
    )(hidden_units, jnp.swapaxes(rank_down, 1, 2), chosen)


def dot_kernel(start, depth, hidden, weight, out, held, arrived):
    width = out.shape[1]
    steps = weight.shape[0] // depth

    def copy(k):
        rows = pl.ds(pl.multiple_of(k * depth, depth), depth)
        return pltpu.make_async_copy(
            weight.at[rows, pl.ds(start, width)], held.at[rows], arrived.at[k]
        )

    @pl.loop(0, steps)
    def _(k):
        copy(k).start()

    out[...] = jnp.zeros_like(out)

    @pl.loop(0, steps)
    def _(k):
        copy(k).wait()
        at = pl.ds(pl.multiple_of(k * depth, depth), depth)
        out[...] += jnp.dot(hidden[:, at], held[at], preferred_element_type=jnp.float32)


def base_term(hidden_units, weight, start, width):
    rows, total_depth = hidden_units.shape
    depth = 768 if total_depth % 768 == 0 else 128 if total_depth % 128 == 0 else total_depth
    return pl.pallas_call(
        functools.partial(dot_kernel, start, depth),
        out_shape=jax.ShapeDtypeStruct((rows, width), jnp.float32),
        in_specs=[pl.BlockSpec(memory_space=pltpu.VMEM), pl.BlockSpec(memory_space=pl.ANY)],
        out_specs=pl.BlockSpec(memory_space=pltpu.VMEM),
        scratch_shapes=[
            pltpu.VMEM((total_depth, width), weight.dtype),
            pltpu.SemaphoreType.DMA((total_depth // depth,)),
        ],
        compiler_params=pltpu.CompilerParams(vmem_limit_bytes=40 << 20),
        cost_estimate=pl.CostEstimate(
            flops=2 * rows * total_depth * width,
            bytes_accessed=2 * total_depth * width,
            transcendentals=0,
        ),
        name="base_dot",
    )(hidden_units, weight)


def gathered_low_rank(partial_low):
    n_tp, n_page, n_sub = (lax.axis_size(axis) for axis in ("tp",) + PS)
    n_ps = n_page * n_sub
    if n_tp != n_ps:
        return lax.psum(partial_low, ("tp",) + PS).astype(jnp.bfloat16)
    pairs = [(t * n_ps + a, a * n_ps + t) for t in range(n_tp) for a in range(n_ps)]
    got = lax.ppermute(partial_low, ("tp",) + PS, pairs)
    spread = lax.all_to_all(
        jnp.broadcast_to(got[None], (n_ps,) + got.shape), PS, split_axis=0, concat_axis=0
    )
    return jnp.sum(spread, axis=0).astype(jnp.bfloat16)


def on_device(hidden_units, adapter_ids, down_projection_weight, rank_down, rank_up, residual):
    n_tp = lax.axis_size("tp")
    owned_count = rank_down.shape[0]
    first_owned = lax.axis_index(PS) * owned_count
    chosen = (
        (adapter_ids - first_owned)[:, None] == jnp.arange(owned_count, dtype=jnp.int32)[None, :]
    ).astype(jnp.float32)
    low_rank = gathered_low_rank(partial_low_rank(hidden_units, rank_down, chosen))
    held_count, rank_width, columns = rank_up.shape
    first_held = lax.axis_index("tp") * held_count
    flattened = rank_up.reshape(held_count * rank_width, columns)
    rows_dev = residual.shape[0]
    picked = (
        (adapter_ids - first_held)[:, None] == jnp.arange(held_count, dtype=jnp.int32)[None, :]
    ).astype(jnp.bfloat16)
    coefficient = (picked[:, :, None] * low_rank[:, None, :]).reshape(
        n_tp * rows_dev, held_count * rank_width
    )
    pieces = []
    start = 0
    widths = CHUNKS if sum(CHUNKS) == columns else (columns,)
    for width in widths:
        at = slice(start, start + width)
        base = base_term(hidden_units, down_projection_weight, start, width)
        term = (
            base + jnp.dot(coefficient, flattened[:, at], preferred_element_type=jnp.float32)
        ).astype(jnp.bfloat16)
        if n_tp > 4:
            summed = lax.psum_scatter(term, "tp", scatter_dimension=0, tiled=True).astype(
                jnp.float32
            )
        else:
            got = lax.all_to_all(
                term.reshape(n_tp, rows_dev, width), "tp", split_axis=0, concat_axis=0
            )
            summed = jnp.sum(got.astype(jnp.float32), axis=0)
        pieces.append((residual[:, at].astype(jnp.float32) + summed).astype(jnp.bfloat16))
        start += width
    return jnp.concatenate(pieces, axis=1)


def solution(mesh):
    placed = (
        P("parts", "tp"),
        P("parts"),
        P("tp", ("page", "sub")),
        P(("parts", "page", "sub"), "tp", None),
        P(("parts", "tp"), None, ("page", "sub")),
        P(("parts", "tp"), ("page", "sub")),
    )
    return jax.shard_map(
        on_device,
        mesh=mesh,
        in_specs=placed,
        out_specs=P(("parts", "tp"), ("page", "sub")),
        check_vma=False,
    )
```

```python
import functools

import jax
import jax.numpy as jnp
from jax import lax
from jax.experimental import pallas as pl
from jax.experimental.pallas import tpu as pltpu
from jax.sharding import PartitionSpec as P

WIDTHS = (1024, 1280, 768)
DEPTH = 768
PS = ("page", "sub")
VMEM = pl.BlockSpec(memory_space=pltpu.VMEM)
HBM = pl.BlockSpec(memory_space=pltpu.HBM)


def column_of(ids_row):
    rows = ids_row.shape[1]
    down = lax.broadcasted_iota(jnp.int32, (rows, rows), 0)
    across = lax.broadcasted_iota(jnp.int32, (rows, rows), 1)
    spread = jnp.broadcast_to(ids_row, (rows, rows))
    return jnp.sum(
        jnp.where(down == across, spread.astype(jnp.float32), 0.0), axis=1, keepdims=True
    )


def deep(k):
    return pl.ds(pl.multiple_of(k * DEPTH, DEPTH), DEPTH)


def weight_copies(weight, held, arrived, start, width):
    def copy(k):
        return pltpu.make_async_copy(
            weight.at[deep(k), pl.ds(start, width)], held.at[deep(k)], arrived.at[k]
        )

    return copy


def first_kernel(
    start,
    width,
    hidden,
    rank_down,
    weight,
    low,
    base,
    hidden_here,
    down_here,
    held,
    got,
    arrived,
):
    steps = weight.shape[0] // DEPTH
    copy = weight_copies(weight, held, arrived, start, width)

    def hidden_copy(k):
        return pltpu.make_async_copy(
            hidden.at[:, deep(k)], hidden_here.at[:, deep(k)], got.at[0, k]
        )

    def down_copy(k):
        return pltpu.make_async_copy(
            rank_down.at[:, deep(k)], down_here.at[:, deep(k)], got.at[1, k]
        )

    @pl.loop(0, steps)
    def _(k):
        hidden_copy(k).start()
        down_copy(k).start()

    @pl.loop(0, steps)
    def _(k):
        copy(k).start()

    low[...] = jnp.zeros_like(low)
    base[...] = jnp.zeros_like(base)

    @pl.loop(0, steps)
    def _(k):
        hidden_copy(k).wait()
        down_copy(k).wait()
        low[...] += lax.dot_general(
            hidden_here[:, deep(k)],
            down_here[:, deep(k)],
            (((1,), (1,)), ((), ())),
            preferred_element_type=jnp.float32,
        )

    @pl.loop(0, steps)
    def _(k):
        copy(k).wait()
        base[...] += jnp.dot(
            hidden_here[:, deep(k)], held[deep(k)], preferred_element_type=jnp.float32
        )


def first_phase(hidden, rank_down, weight, start, width):
    rows, depth = hidden.shape
    rank = rank_down.shape[0]
    steps = depth // DEPTH
    return pl.pallas_call(
        functools.partial(first_kernel, start, width),
        out_shape=(
            jax.ShapeDtypeStruct((rows, rank), jnp.float32),
            jax.ShapeDtypeStruct((rows, width), jnp.float32),
            jax.ShapeDtypeStruct(hidden.shape, hidden.dtype),
        ),
        in_specs=[HBM] * 3,
        out_specs=(VMEM, VMEM, VMEM),
        scratch_shapes=[
            pltpu.VMEM(rank_down.shape, rank_down.dtype),
            pltpu.VMEM((depth, width), weight.dtype),
            pltpu.SemaphoreType.DMA((2, steps)),
            pltpu.SemaphoreType.DMA((steps,)),
        ],
        compiler_params=pltpu.CompilerParams(vmem_limit_bytes=52 << 20),
        cost_estimate=pl.CostEstimate(
            flops=2 * rows * depth * (width + rank),
            bytes_accessed=2 * depth * (width + rank + rows),
            transcendentals=0,
        ),
        name="low_rank_and_base",
    )(hidden, rank_down, weight)


def stream_dot(hidden, weight, total, held, arrived, start):
    steps = weight.shape[0] // DEPTH
    copy = weight_copies(weight, held, arrived, start, total.shape[1])

    @pl.loop(0, steps)
    def _(k):
        copy(k).start()

    total[...] = jnp.zeros_like(total)

    @pl.loop(0, steps)
    def _(k):
        copy(k).wait()
        total[...] += jnp.dot(hidden[:, deep(k)], held[deep(k)], preferred_element_type=jnp.float32)


def base_kernel(start, hidden, weight, base, held, arrived):
    stream_dot(hidden, weight, base, held, arrived, start)


def base_phase(hidden, weight, start, width):
    rows, depth = hidden.shape
    return pl.pallas_call(
        functools.partial(base_kernel, start),
        out_shape=jax.ShapeDtypeStruct((rows, width), jnp.float32),
        in_specs=[VMEM, HBM],
        out_specs=VMEM,
        scratch_shapes=[
            pltpu.VMEM((depth, width), weight.dtype),
            pltpu.SemaphoreType.DMA((depth // DEPTH,)),
        ],
        compiler_params=pltpu.CompilerParams(vmem_limit_bytes=32 << 20),
        cost_estimate=pl.CostEstimate(
            flops=2 * rows * depth * width, bytes_accessed=2 * depth * width, transcendentals=0
        ),
        name="base",
    )(hidden, weight)


def split_rows(total, at, sent, kept):
    block = total.shape[0] // 4
    bit = lax.rem(lax.axis_index("tp"), 2)
    for half in range(2):
        rows = pl.ds(half * block, block)
        there = pl.ds(pl.multiple_of((2 * half + 1 - bit) * block, block), block)
        here = pl.ds(pl.multiple_of((2 * half + bit) * block, block), block)
        sent[rows, at] = total[there, :].astype(sent.dtype)
        kept[rows, at] = total[here, :]


def adapter_term(low, up):
    return jnp.dot(low.astype(jnp.bfloat16), up, preferred_element_type=jnp.float32)


def correct_kernel(ids, low_a, low_b, low_c, low_d, up, base_one, base_two, low, sent, kept, total):
    held = column_of(ids[...]) == lax.axis_index("tp").astype(jnp.float32)
    low[...] = jnp.where(held, (low_a[...] + low_b[...]) + (low_c[...] + low_d[...]), 0.0)
    start = 0
    for base in (base_one, base_two):
        width = base.shape[1]
        at = slice(start, start + width)
        total[:, at] = base[...] + adapter_term(low[...], up[:, at])
        start += width
    split_rows(total, slice(0, start), sent, kept)


def correct_phase(ids, lows, up, base_one, base_two):
    rows, rank = lows[0].shape
    width = base_one.shape[1] + base_two.shape[1]
    return pl.pallas_call(
        correct_kernel,
        out_shape=(
            jax.ShapeDtypeStruct((rows, rank), jnp.float32),
            jax.ShapeDtypeStruct((rows // 2, width), jnp.bfloat16),
            jax.ShapeDtypeStruct((rows // 2, width), jnp.float32),
        ),
        in_specs=[VMEM] * 8,
        out_specs=(VMEM,) * 3,
        scratch_shapes=[pltpu.VMEM((rows, width), jnp.float32)],
        compiler_params=pltpu.CompilerParams(vmem_limit_bytes=8 << 20),
        name="adapter_term",
    )(ids, *lows, up, base_one, base_two)


def last_kernel(start, hidden, weight, low, up, sent, kept, total, held, arrived):
    stream_dot(hidden, weight, total, held, arrived, start)
    width = total.shape[1]
    total[...] += adapter_term(low[...], up[:, start : start + width])
    split_rows(total, slice(0, width), sent, kept)


def last_phase(hidden, weight, low, up, start, width):
    rows, depth = hidden.shape
    return pl.pallas_call(
        functools.partial(last_kernel, start),
        out_shape=(
            jax.ShapeDtypeStruct((rows // 2, width), jnp.bfloat16),
            jax.ShapeDtypeStruct((rows // 2, width), jnp.float32),
        ),
        in_specs=[VMEM, HBM, VMEM, VMEM],
        out_specs=(VMEM, VMEM),
        scratch_shapes=[
            pltpu.VMEM((rows, width), jnp.float32),
            pltpu.VMEM((depth, width), weight.dtype),
            pltpu.SemaphoreType.DMA((depth // DEPTH,)),
        ],
        compiler_params=pltpu.CompilerParams(vmem_limit_bytes=32 << 20),
        cost_estimate=pl.CostEstimate(
            flops=2 * rows * depth * width, bytes_accessed=2 * depth * width, transcendentals=0
        ),
        name="last_base",
    )(hidden, weight, low, up)


def pair_kernel(kept, got, sent, total):
    block = kept.shape[0] // 2
    high = lax.div(lax.axis_index("tp"), 2)
    here = pl.ds(pl.multiple_of(high * block, block), block)
    there = pl.ds(pl.multiple_of((1 - high) * block, block), block)
    sent[...] = (kept[there, :] + got[there, :].astype(jnp.float32)).astype(sent.dtype)
    total[...] = kept[here, :] + got[here, :].astype(jnp.float32)


def pair_phase(kept, got):
    rows, width = kept.shape
    return pl.pallas_call(
        pair_kernel,
        out_shape=(
            jax.ShapeDtypeStruct((rows // 2, width), jnp.bfloat16),
            jax.ShapeDtypeStruct((rows // 2, width), jnp.float32),
        ),
        in_specs=[VMEM] * 2,
        out_specs=(VMEM,) * 2,
        compiler_params=pltpu.CompilerParams(vmem_limit_bytes=8 << 20),
        name="pair_sum",
    )(kept, got)


def finish_kernel(residual, total_one, got_one, total_two, got_two, mixed):
    start = 0
    for total, got in ((total_one, got_one), (total_two, got_two)):
        at = slice(start, start + total.shape[1])
        mixed[:, at] = (
            residual[:, at].astype(jnp.float32) + total[...] + got[...].astype(jnp.float32)
        ).astype(mixed.dtype)
        start = at.stop


def finish_phase(residual, *terms):
    return pl.pallas_call(
        finish_kernel,
        out_shape=jax.ShapeDtypeStruct(residual.shape, residual.dtype),
        in_specs=[VMEM] * 5,
        out_specs=VMEM,
        compiler_params=pltpu.CompilerParams(vmem_limit_bytes=8 << 20),
        name="finish",
    )(residual, *terms)


def swap(value, bit):
    return lax.ppermute(value, "tp", [(i, i ^ bit) for i in range(lax.axis_size("tp"))])


def four_by_four(hidden_units, adapter_ids, weight, rank_down, rank_up, residual):
    up = rank_up[0]
    one, two, three = WIDTHS
    low, base_one, hidden = first_phase(
        hidden_units, jnp.swapaxes(rank_down, 1, 2)[0], weight, 0, one
    )
    lows = []
    for j in range(4):
        pairs = [(t * 4 + a, a * 4 + (t + j) % 4) for t in range(4) for a in range(4)]
        lows.append(lax.ppermute(low, ("tp",) + PS, pairs))
    base_two = base_phase(hidden, weight, one, two)
    low, sent, kept = correct_phase(adapter_ids[None], lows, up, base_one, base_two)
    got = swap(sent, 1)
    sent_last, kept_last = last_phase(hidden, weight, low, up, one + two, three)
    got_last = swap(sent_last, 1)
    sent, total = pair_phase(kept, got)
    got = swap(sent, 2)
    sent_last, total_last = pair_phase(kept_last, got_last)
    got_last = swap(sent_last, 2)
    return finish_phase(residual, total, got, total_last, got_last)


def any_size(hidden_units, adapter_ids, down_projection_weight, rank_down, rank_up, residual):
    owned_count = rank_down.shape[0]
    first_owned = lax.axis_index(PS) * owned_count
    chosen = (
        (adapter_ids - first_owned)[:, None] == jnp.arange(owned_count, dtype=jnp.int32)[None, :]
    ).astype(jnp.float32)
    projected = jnp.einsum(
        "rf,afk->rak", hidden_units, rank_down, preferred_element_type=jnp.float32
    )
    partial_low = jnp.einsum("rak,ra->rk", projected, chosen)
    low_rank = lax.psum(partial_low, ("tp",) + PS).astype(jnp.bfloat16)
    held_count, rank_width, columns = rank_up.shape
    first_held = lax.axis_index("tp") * held_count
    picked = (
        (adapter_ids - first_held)[:, None] == jnp.arange(held_count, dtype=jnp.int32)[None, :]
    ).astype(jnp.bfloat16)
    coefficient = (picked[:, :, None] * low_rank[:, None, :]).reshape(
        -1, held_count * rank_width
    )
    term = jnp.dot(
        hidden_units, down_projection_weight, preferred_element_type=jnp.float32
    ) + jnp.dot(
        coefficient,
        rank_up.reshape(held_count * rank_width, columns),
        preferred_element_type=jnp.float32,
    )
    summed = lax.psum_scatter(
        term.astype(jnp.bfloat16), "tp", scatter_dimension=0, tiled=True
    ).astype(jnp.float32)
    return (residual.astype(jnp.float32) + summed).astype(jnp.bfloat16)


def on_device(hidden_units, adapter_ids, down_projection_weight, rank_down, rank_up, residual):
    sizes = [lax.axis_size(axis) for axis in ("tp",) + PS]
    fits = (
        sizes[0] == 4
        and sizes[1] * sizes[2] == 4
        and rank_down.shape[0] == 1
        and rank_up.shape[0] == 1
        and residual.shape == (16, sum(WIDTHS))
        and hidden_units.shape[1] % DEPTH == 0
    )
    form = four_by_four if fits else any_size
    return form(hidden_units, adapter_ids, down_projection_weight, rank_down, rank_up, residual)


def solution(mesh):
    placed = (
        P("parts", "tp"),
        P("parts"),
        P("tp", ("page", "sub")),
        P(("parts", "page", "sub"), "tp", None),
        P(("parts", "tp"), None, ("page", "sub")),
        P(("parts", "tp"), ("page", "sub")),
    )
    return jax.shard_map(
        on_device,
        mesh=mesh,
        in_specs=placed,
        out_specs=P(("parts", "tp"), ("page", "sub")),
        check_vma=False,
    )
```

```python
import functools

import jax
import jax.numpy as jnp
from jax import lax
from jax.experimental import pallas as pl
from jax.experimental.pallas import tpu as pltpu
from jax.sharding import PartitionSpec as P

WIDTHS = (1024, 1024, 512, 512)
DEPTH = 768
IN_FLIGHT = 4
PS = ("page", "sub")
VMEM = pl.BlockSpec(memory_space=pltpu.VMEM)
HBM = pl.BlockSpec(memory_space=pltpu.HBM)


def column_of(ids_row):
    rows = ids_row.shape[1]
    down = lax.broadcasted_iota(jnp.int32, (rows, rows), 0)
    across = lax.broadcasted_iota(jnp.int32, (rows, rows), 1)
    spread = jnp.broadcast_to(ids_row, (rows, rows))
    return jnp.sum(
        jnp.where(down == across, spread.astype(jnp.float32), 0.0), axis=1, keepdims=True
    )


def deep(k):
    return pl.ds(pl.multiple_of(k * DEPTH, DEPTH), DEPTH)


def weight_copies(weight, held, arrived, start, width):
    def copy(k):
        return pltpu.make_async_copy(
            weight.at[deep(k), pl.ds(start, width)], held.at[deep(k)], arrived.at[k]
        )

    return copy


def low_kernel(hidden, rank_down, low, hidden_here, down_here, got):
    steps = hidden.shape[1] // DEPTH

    def hidden_copy(k):
        return pltpu.make_async_copy(
            hidden.at[:, deep(k)], hidden_here.at[:, deep(k)], got.at[0, k]
        )

    def down_copy(k):
        return pltpu.make_async_copy(
            rank_down.at[:, deep(k)], down_here.at[:, deep(k)], got.at[1, k]
        )

    @pl.loop(0, steps)
    def _(k):
        hidden_copy(k).start()
        down_copy(k).start()

    low[...] = jnp.zeros_like(low)

    @pl.loop(0, steps)
    def _(k):
        hidden_copy(k).wait()
        down_copy(k).wait()
        low[...] += lax.dot_general(
            hidden_here[:, deep(k)],
            down_here[:, deep(k)],
            (((1,), (1,)), ((), ())),
            preferred_element_type=jnp.float32,
        )


def low_phase(hidden, rank_down):
    rows, depth = hidden.shape
    rank = rank_down.shape[0]
    return pl.pallas_call(
        low_kernel,
        out_shape=(
            jax.ShapeDtypeStruct((rows, rank), jnp.float32),
            jax.ShapeDtypeStruct(hidden.shape, hidden.dtype),
        ),
        in_specs=[HBM] * 2,
        out_specs=(VMEM, VMEM),
        scratch_shapes=[
            pltpu.VMEM(rank_down.shape, rank_down.dtype),
            pltpu.SemaphoreType.DMA((2, depth // DEPTH)),
        ],
        compiler_params=pltpu.CompilerParams(vmem_limit_bytes=52 << 20),
        cost_estimate=pl.CostEstimate(
            flops=2 * rows * depth * rank,
            bytes_accessed=2 * depth * (rank + rows),
            transcendentals=0,
        ),
        name="low_rank",
    )(hidden, rank_down)


def stream_dot(hidden, weight, total, held, arrived, start):
    steps = weight.shape[0] // DEPTH
    copy = weight_copies(weight, held, arrived, start, total.shape[1])

    @pl.loop(0, IN_FLIGHT)
    def _(k):
        copy(k).start()

    total[...] = jnp.zeros_like(total)

    @pl.loop(0, steps)
    def _(k):
        @pl.when(k + IN_FLIGHT < steps)
        def _():
            copy(k + IN_FLIGHT).start()

        copy(k).wait()
        total[...] += jnp.dot(hidden[:, deep(k)], held[deep(k)], preferred_element_type=jnp.float32)


def base_kernel(start, hidden, weight, base, held, arrived):
    stream_dot(hidden, weight, base, held, arrived, start)


def base_phase(hidden, weight, start, width):
    rows, depth = hidden.shape
    return pl.pallas_call(
        functools.partial(base_kernel, start),
        out_shape=jax.ShapeDtypeStruct((rows, width), jnp.float32),
        in_specs=[VMEM, HBM],
        out_specs=VMEM,
        scratch_shapes=[
            pltpu.VMEM((depth, width), weight.dtype),
            pltpu.SemaphoreType.DMA((depth // DEPTH,)),
        ],
        compiler_params=pltpu.CompilerParams(vmem_limit_bytes=32 << 20),
        cost_estimate=pl.CostEstimate(
            flops=2 * rows * depth * width, bytes_accessed=2 * depth * width, transcendentals=0
        ),
        name="base",
    )(hidden, weight)


def split_rows(total, at, sent, kept):
    block = total.shape[0] // 4
    bit = lax.rem(lax.axis_index("tp"), 2)
    for half in range(2):
        rows = pl.ds(half * block, block)
        there = pl.ds(pl.multiple_of((2 * half + 1 - bit) * block, block), block)
        here = pl.ds(pl.multiple_of((2 * half + bit) * block, block), block)
        sent[rows, at] = total[there, :].astype(sent.dtype)
        kept[rows, at] = total[here, :]


def adapter_term(low, up):
    return jnp.dot(low.astype(jnp.bfloat16), up, preferred_element_type=jnp.float32)


def correct_kernel(ids, low_a, low_b, low_c, low_d, up, base_one, base_two, low, sent, kept, total):
    held = column_of(ids[...]) == lax.axis_index("tp").astype(jnp.float32)
    low[...] = jnp.where(held, (low_a[...] + low_b[...]) + (low_c[...] + low_d[...]), 0.0)
    start = 0
    for base in (base_one, base_two):
        width = base.shape[1]
        at = slice(start, start + width)
        total[:, at] = base[...] + adapter_term(low[...], up[:, at])
        start += width
    split_rows(total, slice(0, start), sent, kept)


def correct_phase(ids, lows, up, base_one, base_two):
    rows, rank = lows[0].shape
    width = base_one.shape[1] + base_two.shape[1]
    return pl.pallas_call(
        correct_kernel,
        out_shape=(
            jax.ShapeDtypeStruct((rows, rank), jnp.float32),
            jax.ShapeDtypeStruct((rows // 2, width), jnp.bfloat16),
            jax.ShapeDtypeStruct((rows // 2, width), jnp.float32),
        ),
        in_specs=[VMEM] * 8,
        out_specs=(VMEM,) * 3,
        scratch_shapes=[pltpu.VMEM((rows, width), jnp.float32)],
        compiler_params=pltpu.CompilerParams(vmem_limit_bytes=8 << 20),
        name="adapter_term",
    )(ids, *lows, up, base_one, base_two)


def last_kernel(start, hidden, weight, low, up, base, sent, kept, total, held, arrived):
    before = base.shape[1]
    width = total.shape[1] - before
    stream_dot(hidden, weight, total.at[:, before:], held, arrived, start + before)
    total[:, :before] = base[...]
    total[...] += adapter_term(low[...], up[:, start : start + before + width])
    split_rows(total, slice(0, before + width), sent, kept)


def last_phase(hidden, weight, low, up, base, start, width):
    rows, depth = hidden.shape
    both = base.shape[1] + width
    return pl.pallas_call(
        functools.partial(last_kernel, start),
        out_shape=(
            jax.ShapeDtypeStruct((rows // 2, both), jnp.bfloat16),
            jax.ShapeDtypeStruct((rows // 2, both), jnp.float32),
        ),
        in_specs=[VMEM, HBM, VMEM, VMEM, VMEM],
        out_specs=(VMEM, VMEM),
        scratch_shapes=[
            pltpu.VMEM((rows, both), jnp.float32),
            pltpu.VMEM((depth, width), weight.dtype),
            pltpu.SemaphoreType.DMA((depth // DEPTH,)),
        ],
        compiler_params=pltpu.CompilerParams(vmem_limit_bytes=32 << 20),
        cost_estimate=pl.CostEstimate(
            flops=2 * rows * depth * width, bytes_accessed=2 * depth * width, transcendentals=0
        ),
        name="last_base",
    )(hidden, weight, low, up, base)


def pair_kernel(kept, got, sent, total):
    block = kept.shape[0] // 2
    high = lax.div(lax.axis_index("tp"), 2)
    here = pl.ds(pl.multiple_of(high * block, block), block)
    there = pl.ds(pl.multiple_of((1 - high) * block, block), block)
    sent[...] = (kept[there, :] + got[there, :].astype(jnp.float32)).astype(sent.dtype)
    total[...] = kept[here, :] + got[here, :].astype(jnp.float32)


def pair_phase(kept, got):
    rows, width = kept.shape
    return pl.pallas_call(
        pair_kernel,
        out_shape=(
            jax.ShapeDtypeStruct((rows // 2, width), jnp.bfloat16),
            jax.ShapeDtypeStruct((rows // 2, width), jnp.float32),
        ),
        in_specs=[VMEM] * 2,
        out_specs=(VMEM,) * 2,
        compiler_params=pltpu.CompilerParams(vmem_limit_bytes=8 << 20),
        name="pair_sum",
    )(kept, got)


def finish_kernel(residual, total_one, got_one, total_two, got_two, mixed):
    start = 0
    for total, got in ((total_one, got_one), (total_two, got_two)):
        at = slice(start, start + total.shape[1])
        mixed[:, at] = (
            residual[:, at].astype(jnp.float32) + total[...] + got[...].astype(jnp.float32)
        ).astype(mixed.dtype)
        start = at.stop


def finish_phase(residual, *terms):
    return pl.pallas_call(
        finish_kernel,
        out_shape=jax.ShapeDtypeStruct(residual.shape, residual.dtype),
        in_specs=[VMEM] * 5,
        out_specs=VMEM,
        compiler_params=pltpu.CompilerParams(vmem_limit_bytes=8 << 20),
        name="finish",
    )(residual, *terms)


def swap(value, bit):
    return lax.ppermute(value, "tp", [(i, i ^ bit) for i in range(lax.axis_size("tp"))])


def four_by_four(hidden_units, adapter_ids, weight, rank_down, rank_up, residual):
    up = rank_up[0]
    one, two, three, four = WIDTHS
    low, hidden = low_phase(hidden_units, jnp.swapaxes(rank_down, 1, 2)[0])
    pairs = [(t * 4 + a, a * 4 + t) for t in range(4) for a in range(4)]
    low = lax.ppermute(low, ("tp",) + PS, pairs)
    base_one = base_phase(hidden, weight, 0, one)
    hidden, low, base_one = lax.optimization_barrier((hidden, low, base_one))
    lows = [low] + [
        lax.ppermute(low, PS, [(i, i ^ other) for i in range(4)]) for other in (2, 3, 1)
    ]
    base_two = base_phase(hidden, weight, one, two)
    low, sent, kept = correct_phase(adapter_ids[None], lows, up, base_one, base_two)
    got = swap(sent, 1)
    hidden, low = lax.optimization_barrier((hidden, low))
    base_three = base_phase(hidden, weight, one + two, three)
    kept, got, base_three = lax.optimization_barrier((kept, got, base_three))
    sent, total = pair_phase(kept, got)
    got = swap(sent, 2)
    hidden, total = lax.optimization_barrier((hidden, total))
    sent_last, kept_last = last_phase(hidden, weight, low, up, base_three, one + two, four)
    got_last = swap(sent_last, 1)
    sent_last, total_last = pair_phase(kept_last, got_last)
    got_last = swap(sent_last, 2)
    return finish_phase(residual, total, got, total_last, got_last)


def any_size(hidden_units, adapter_ids, down_projection_weight, rank_down, rank_up, residual):
    owned_count = rank_down.shape[0]
    first_owned = lax.axis_index(PS) * owned_count
    chosen = (
        (adapter_ids - first_owned)[:, None] == jnp.arange(owned_count, dtype=jnp.int32)[None, :]
    ).astype(jnp.float32)
    projected = jnp.einsum(
        "rf,afk->rak", hidden_units, rank_down, preferred_element_type=jnp.float32
    )
    partial_low = jnp.einsum("rak,ra->rk", projected, chosen)
    low_rank = lax.psum(partial_low, ("tp",) + PS).astype(jnp.bfloat16)
    held_count, rank_width, columns = rank_up.shape
    first_held = lax.axis_index("tp") * held_count
    picked = (
        (adapter_ids - first_held)[:, None] == jnp.arange(held_count, dtype=jnp.int32)[None, :]
    ).astype(jnp.bfloat16)
    coefficient = (picked[:, :, None] * low_rank[:, None, :]).reshape(
        -1, held_count * rank_width
    )
    term = jnp.dot(
        hidden_units, down_projection_weight, preferred_element_type=jnp.float32
    ) + jnp.dot(
        coefficient,
        rank_up.reshape(held_count * rank_width, columns),
        preferred_element_type=jnp.float32,
    )
    summed = lax.psum_scatter(
        term.astype(jnp.bfloat16), "tp", scatter_dimension=0, tiled=True
    ).astype(jnp.float32)
    return (residual.astype(jnp.float32) + summed).astype(jnp.bfloat16)


def on_device(hidden_units, adapter_ids, down_projection_weight, rank_down, rank_up, residual):
    sizes = [lax.axis_size(axis) for axis in ("tp",) + PS]
    fits = (
        sizes[0] == 4
        and sizes[1] * sizes[2] == 4
        and rank_down.shape[0] == 1
        and rank_up.shape[0] == 1
        and residual.shape == (16, sum(WIDTHS))
        and hidden_units.shape[1] % DEPTH == 0
    )
    form = four_by_four if fits else any_size
    return form(hidden_units, adapter_ids, down_projection_weight, rank_down, rank_up, residual)


def solution(mesh):
    placed = (
        P("parts", "tp"),
        P("parts"),
        P("tp", ("page", "sub")),
        P(("parts", "page", "sub"), "tp", None),
        P(("parts", "tp"), None, ("page", "sub")),
        P(("parts", "tp"), ("page", "sub")),
    )
    return jax.shard_map(
        on_device,
        mesh=mesh,
        in_specs=placed,
        out_specs=P(("parts", "tp"), ("page", "sub")),
        check_vma=False,
    )
```

```python
import functools

import jax
import jax.numpy as jnp
from jax import lax
from jax.experimental import pallas as pl
from jax.experimental.pallas import tpu as pltpu
from jax.sharding import PartitionSpec as P

WIDTHS = (1280, 1280, 512)
DEPTH = 768
PS = ("page", "sub")
VMEM = pl.BlockSpec(memory_space=pltpu.VMEM)
HBM = pl.BlockSpec(memory_space=pltpu.HBM)


def column_of(ids_row):
    rows = ids_row.shape[1]
    down = lax.broadcasted_iota(jnp.int32, (rows, rows), 0)
    across = lax.broadcasted_iota(jnp.int32, (rows, rows), 1)
    spread = jnp.broadcast_to(ids_row, (rows, rows))
    return jnp.sum(
        jnp.where(down == across, spread.astype(jnp.float32), 0.0), axis=1, keepdims=True
    )


def deep(k):
    return pl.ds(pl.multiple_of(k * DEPTH, DEPTH), DEPTH)


def weight_copies(weight, held, arrived, start, width):
    def copy(k):
        return pltpu.make_async_copy(
            weight.at[deep(k), pl.ds(start, width)], held.at[deep(k)], arrived.at[k]
        )

    return copy


def first_kernel(
    start,
    width,
    hidden,
    rank_down,
    weight,
    packed,
    base,
    hidden_here,
    low,
    down_here,
    held,
    got,
    arrived,
):
    steps = weight.shape[0] // DEPTH
    copy = weight_copies(weight, held, arrived, start, width)

    def hidden_copy(k):
        return pltpu.make_async_copy(
            hidden.at[:, deep(k)], hidden_here.at[:, deep(k)], got.at[0, k]
        )

    def down_copy(k):
        return pltpu.make_async_copy(
            rank_down.at[:, deep(k)], down_here.at[:, deep(k)], got.at[1, k]
        )

    @pl.loop(0, steps)
    def _(k):
        hidden_copy(k).start()
        down_copy(k).start()

    @pl.loop(0, steps)
    def _(k):
        copy(k).start()

    low[...] = jnp.zeros_like(low)
    base[...] = jnp.zeros_like(base)

    @pl.loop(0, steps)
    def _(k):
        hidden_copy(k).wait()
        down_copy(k).wait()
        low[...] += lax.dot_general(
            hidden_here[:, deep(k)],
            down_here[:, deep(k)],
            (((1,), (1,)), ((), ())),
            preferred_element_type=jnp.float32,
        )

    half = low.shape[0] // 2
    block = jnp.concatenate([low[:half, :], low[half:, :]], axis=1)
    for to in range(packed.shape[0]):
        packed[to] = block

    @pl.loop(0, steps)
    def _(k):
        copy(k).wait()
        base[...] += jnp.dot(
            hidden_here[:, deep(k)], held[deep(k)], preferred_element_type=jnp.float32
        )


def first_phase(hidden, rank_down, weight, start, width):
    rows, depth = hidden.shape
    rank = rank_down.shape[0]
    steps = depth // DEPTH
    return pl.pallas_call(
        functools.partial(first_kernel, start, width),
        out_shape=(
            jax.ShapeDtypeStruct((16, rows // 2, 2 * rank), jnp.float32),
            jax.ShapeDtypeStruct((rows, width), jnp.float32),
            jax.ShapeDtypeStruct(hidden.shape, hidden.dtype),
        ),
        in_specs=[HBM] * 3,
        out_specs=(VMEM, VMEM, VMEM),
        scratch_shapes=[
            pltpu.VMEM((rows, rank), jnp.float32),
            pltpu.VMEM(rank_down.shape, rank_down.dtype),
            pltpu.VMEM((depth, width), weight.dtype),
            pltpu.SemaphoreType.DMA((2, steps)),
            pltpu.SemaphoreType.DMA((steps,)),
        ],
        compiler_params=pltpu.CompilerParams(vmem_limit_bytes=52 << 20),
        cost_estimate=pl.CostEstimate(
            flops=2 * rows * depth * (width + rank),
            bytes_accessed=2 * depth * (width + rank + rows),
            transcendentals=0,
        ),
        name="low_rank_and_base",
    )(hidden, rank_down, weight)


def stream_dot(hidden, weight, total, held, arrived, start):
    steps = weight.shape[0] // DEPTH
    copy = weight_copies(weight, held, arrived, start, total.shape[1])

    @pl.loop(0, steps)
    def _(k):
        copy(k).start()

    total[...] = jnp.zeros_like(total)

    @pl.loop(0, steps)
    def _(k):
        copy(k).wait()
        total[...] += jnp.dot(hidden[:, deep(k)], held[deep(k)], preferred_element_type=jnp.float32)


def base_kernel(start, hidden, weight, base, held, arrived):
    stream_dot(hidden, weight, base, held, arrived, start)


def base_phase(hidden, weight, start, width):
    rows, depth = hidden.shape
    return pl.pallas_call(
        functools.partial(base_kernel, start),
        out_shape=jax.ShapeDtypeStruct((rows, width), jnp.float32),
        in_specs=[VMEM, HBM],
        out_specs=VMEM,
        scratch_shapes=[
            pltpu.VMEM((depth, width), weight.dtype),
            pltpu.SemaphoreType.DMA((depth // DEPTH,)),
        ],
        compiler_params=pltpu.CompilerParams(vmem_limit_bytes=32 << 20),
        cost_estimate=pl.CostEstimate(
            flops=2 * rows * depth * width, bytes_accessed=2 * depth * width, transcendentals=0
        ),
        name="base",
    )(hidden, weight)


def split_rows(total, at, sent, kept):
    block = total.shape[0] // 4
    bit = lax.rem(lax.axis_index("tp"), 2)
    for half in range(2):
        rows = pl.ds(half * block, block)
        there = pl.ds(pl.multiple_of((2 * half + 1 - bit) * block, block), block)
        here = pl.ds(pl.multiple_of((2 * half + bit) * block, block), block)
        sent[rows, at] = total[there, :].astype(sent.dtype)
        kept[rows, at] = total[here, :]


def adapter_term(low, up):
    return jnp.dot(low.astype(jnp.bfloat16), up, preferred_element_type=jnp.float32)


def correct_kernel(ids, packed, up, base_one, base_two, low, sent, kept, total):
    tp = lax.axis_index("tp")
    summed = packed[tp]
    for source in range(1, 4):
        summed = summed + packed[4 * source + tp]
    rank = low.shape[1]
    summed = jnp.concatenate([summed[:, :rank], summed[:, rank:]], axis=0)
    held = column_of(ids[...]) == tp.astype(jnp.float32)
    low[...] = jnp.where(held, summed, 0.0)
    start = 0
    for base in (base_one, base_two):
        width = base.shape[1]
        at = slice(start, start + width)
        total[:, at] = base[...] + adapter_term(low[...], up[:, at])
        start += width
    split_rows(total, slice(0, start), sent, kept)


def correct_phase(ids, packed, up, base_one, base_two):
    rows = base_one.shape[0]
    rank = up.shape[0]
    width = base_one.shape[1] + base_two.shape[1]
    return pl.pallas_call(
        correct_kernel,
        out_shape=(
            jax.ShapeDtypeStruct((rows, rank), jnp.float32),
            jax.ShapeDtypeStruct((rows // 2, width), jnp.bfloat16),
            jax.ShapeDtypeStruct((rows // 2, width), jnp.float32),
        ),
        in_specs=[VMEM] * 5,
        out_specs=(VMEM,) * 3,
        scratch_shapes=[pltpu.VMEM((rows, width), jnp.float32)],
        compiler_params=pltpu.CompilerParams(vmem_limit_bytes=8 << 20),
        name="adapter_term",
    )(ids, packed, up, base_one, base_two)


def last_kernel(start, hidden, weight, low, up, total, held, arrived):
    stream_dot(hidden, weight, total, held, arrived, start)
    total[...] += adapter_term(low[...], up[:, start : start + total.shape[1]])


def last_phase(hidden, weight, low, up, start, width):
    rows, depth = hidden.shape
    return pl.pallas_call(
        functools.partial(last_kernel, start),
        out_shape=jax.ShapeDtypeStruct((rows, width), jnp.float32),
        in_specs=[VMEM, HBM, VMEM, VMEM],
        out_specs=VMEM,
        scratch_shapes=[
            pltpu.VMEM((depth, width), weight.dtype),
            pltpu.SemaphoreType.DMA((depth // DEPTH,)),
        ],
        compiler_params=pltpu.CompilerParams(vmem_limit_bytes=32 << 20),
        cost_estimate=pl.CostEstimate(
            flops=2 * rows * depth * width, bytes_accessed=2 * depth * width, transcendentals=0
        ),
        name="last_base",
    )(hidden, weight, low, up)


def join_kernel(kept, got, last, residual, to_one, to_two, to_three, total):
    block = residual.shape[0]
    before = kept.shape[1]
    tp = lax.axis_index("tp")
    high, low = lax.div(tp, 2), lax.rem(tp, 2)

    def rows(index):
        return pl.ds(pl.multiple_of(index * block, block), block)

    def pair(half):
        return kept[rows(half), :] + got[rows(half), :].astype(jnp.float32)

    to_two[:, :before] = pair(1 - high).astype(to_two.dtype)
    to_two[:, before:] = last[rows(2 * (1 - high) + low), :].astype(to_two.dtype)
    to_one[...] = last[rows(2 * high + 1 - low), :].astype(to_one.dtype)
    to_three[...] = last[rows(3 - tp), :].astype(to_three.dtype)
    total[:, :before] = residual[:, :before].astype(jnp.float32) + pair(high)
    total[:, before:] = residual[:, before:].astype(jnp.float32) + last[rows(tp), :]


def join_phase(kept, got, last, residual):
    block, width = residual.shape
    return pl.pallas_call(
        join_kernel,
        out_shape=(
            jax.ShapeDtypeStruct((block, last.shape[1]), jnp.bfloat16),
            jax.ShapeDtypeStruct((block, width), jnp.bfloat16),
            jax.ShapeDtypeStruct((block, last.shape[1]), jnp.bfloat16),
            jax.ShapeDtypeStruct((block, width), jnp.float32),
        ),
        in_specs=[VMEM] * 4,
        out_specs=(VMEM,) * 4,
        compiler_params=pltpu.CompilerParams(vmem_limit_bytes=8 << 20),
        name="join",
    )(kept, got, last, residual)


def finish_kernel(total, one, two, three, mixed):
    before = total.shape[1] - one.shape[1]
    mixed[:, :before] = (total[:, :before] + two[:, :before].astype(jnp.float32)).astype(
        mixed.dtype
    )
    mixed[:, before:] = (
        total[:, before:]
        + two[:, before:].astype(jnp.float32)
        + (one[...].astype(jnp.float32) + three[...].astype(jnp.float32))
    ).astype(mixed.dtype)


def finish_phase(total, one, two, three):
    return pl.pallas_call(
        finish_kernel,
        out_shape=jax.ShapeDtypeStruct(total.shape, two.dtype),
        in_specs=[VMEM] * 4,
        out_specs=VMEM,
        compiler_params=pltpu.CompilerParams(vmem_limit_bytes=8 << 20),
        name="finish",
    )(total, one, two, three)


def swap(value, bit):
    return lax.ppermute(value, "tp", [(i, i ^ bit) for i in range(lax.axis_size("tp"))])


def four_by_four(hidden_units, adapter_ids, weight, rank_down, rank_up, residual):
    up = rank_up[0]
    one, two, three = WIDTHS
    packed, base_one, hidden = first_phase(
        hidden_units, jnp.swapaxes(rank_down, 1, 2)[0], weight, 0, one
    )
    packed = lax.all_to_all(packed, ("tp",) + PS, split_axis=0, concat_axis=0, tiled=True)
    base_two = base_phase(hidden, weight, one, two)
    low, sent, kept = correct_phase(adapter_ids[None], packed, up, base_one, base_two)
    got = swap(sent, 1)
    last = last_phase(hidden, weight, low, up, one + two, three)
    to_one, to_two, to_three, total = join_phase(kept, got, last, residual)
    return finish_phase(total, swap(to_one, 1), swap(to_two, 2), swap(to_three, 3))


def any_size(hidden_units, adapter_ids, down_projection_weight, rank_down, rank_up, residual):
    owned_count = rank_down.shape[0]
    first_owned = lax.axis_index(PS) * owned_count
    chosen = (
        (adapter_ids - first_owned)[:, None] == jnp.arange(owned_count, dtype=jnp.int32)[None, :]
    ).astype(jnp.float32)
    projected = jnp.einsum(
        "rf,afk->rak", hidden_units, rank_down, preferred_element_type=jnp.float32
    )
    partial_low = jnp.einsum("rak,ra->rk", projected, chosen)
    low_rank = lax.psum(partial_low, ("tp",) + PS).astype(jnp.bfloat16)
    held_count, rank_width, columns = rank_up.shape
    first_held = lax.axis_index("tp") * held_count
    picked = (
        (adapter_ids - first_held)[:, None] == jnp.arange(held_count, dtype=jnp.int32)[None, :]
    ).astype(jnp.bfloat16)
    coefficient = (picked[:, :, None] * low_rank[:, None, :]).reshape(
        -1, held_count * rank_width
    )
    term = jnp.dot(
        hidden_units, down_projection_weight, preferred_element_type=jnp.float32
    ) + jnp.dot(
        coefficient,
        rank_up.reshape(held_count * rank_width, columns),
        preferred_element_type=jnp.float32,
    )
    summed = lax.psum_scatter(
        term.astype(jnp.bfloat16), "tp", scatter_dimension=0, tiled=True
    ).astype(jnp.float32)
    return (residual.astype(jnp.float32) + summed).astype(jnp.bfloat16)


def on_device(hidden_units, adapter_ids, down_projection_weight, rank_down, rank_up, residual):
    sizes = [lax.axis_size(axis) for axis in ("tp",) + PS]
    fits = (
        sizes[0] == 4
        and sizes[1] * sizes[2] == 4
        and rank_down.shape[0] == 1
        and rank_up.shape[0] == 1
        and residual.shape == (16, sum(WIDTHS))
        and hidden_units.shape[1] % DEPTH == 0
    )
    form = four_by_four if fits else any_size
    return form(hidden_units, adapter_ids, down_projection_weight, rank_down, rank_up, residual)


def solution(mesh):
    placed = (
        P("parts", "tp"),
        P("parts"),
        P("tp", ("page", "sub")),
        P(("parts", "page", "sub"), "tp", None),
        P(("parts", "tp"), None, ("page", "sub")),
        P(("parts", "tp"), ("page", "sub")),
    )
    return jax.shard_map(
        on_device,
        mesh=mesh,
        in_specs=placed,
        out_specs=P(("parts", "tp"), ("page", "sub")),
        check_vma=False,
    )
```

```python
import functools

import jax
import jax.numpy as jnp
from jax import lax
from jax.experimental import pallas as pl
from jax.experimental.pallas import tpu as pltpu
from jax.sharding import PartitionSpec as P

PART = 256
GROUP = 3
SLOTS = 6
TILE = 512
PS = ("page", "sub")
VMEM = pl.BlockSpec(memory_space=pltpu.VMEM)
HBM = pl.BlockSpec(memory_space=pltpu.HBM)


def column_of(ids_row):
    rows = ids_row.shape[1]
    down = lax.broadcasted_iota(jnp.int32, (rows, rows), 0)
    across = lax.broadcasted_iota(jnp.int32, (rows, rows), 1)
    spread = jnp.broadcast_to(ids_row, (rows, rows))
    return jnp.sum(
        jnp.where(down == across, spread.astype(jnp.float32), 0.0), axis=1, keepdims=True
    )


def stream_kernel(
    ids, hidden, rank_down, weight, low, sent, kept, ids_here, hidden_here, down_here, total, held, got, arrived
):
    groups = weight.shape[0] // (PART * GROUP)
    width = weight.shape[1]
    deep = PART * GROUP

    def part_copy(group, part):
        rows = pl.ds(pl.multiple_of(group * deep + part * PART, PART), PART)
        slot = lax.rem(group, SLOTS)
        there = pl.ds(pl.multiple_of(slot * deep + part * PART, PART), PART)
        return pltpu.make_async_copy(
            weight.at[rows], held.at[there], arrived.at[slot * GROUP + part]
        )

    first = [
        pltpu.make_async_copy(hidden, hidden_here, got.at[0]),
        pltpu.make_async_copy(rank_down, down_here, got.at[1]),
        pltpu.make_async_copy(ids, ids_here, got.at[2]),
    ]
    for copy in first:
        copy.start()

    @pl.loop(0, SLOTS - 1)
    def _(group):
        for part in range(GROUP):
            part_copy(group, part).start()

    total[...] = jnp.zeros_like(total)
    for copy in first:
        copy.wait()
    owned = lax.axis_index("page") * lax.axis_size("sub") + lax.axis_index("sub")
    mine = column_of(ids_here[...]) == owned.astype(jnp.float32)
    product = lax.dot_general(
        hidden_here[...],
        down_here[...],
        (((1,), (1,)), ((), ())),
        preferred_element_type=jnp.float32,
    )
    low[...] = jnp.where(mine, product, 0.0)

    def add(group, part, depth):
        at = pl.ds(pl.multiple_of(group * deep + part * PART, PART), depth)
        slot = pl.ds(pl.multiple_of(lax.rem(group, SLOTS) * deep + part * PART, PART), depth)
        for start in range(0, width, TILE):
            columns = slice(start, start + TILE)
            total[:, columns] += jnp.dot(
                hidden_here[:, at], held[slot, columns], preferred_element_type=jnp.float32
            )

    @pl.loop(0, groups - 1)
    def _(group):
        @pl.when(group + SLOTS - 1 < groups)
        def _():
            for part in range(GROUP):
                part_copy(group + SLOTS - 1, part).start()

        for part in range(GROUP):
            part_copy(group, part).wait()
        add(group, 0, deep)

    for part in range(GROUP):
        part_copy(groups - 1, part).wait()
        add(groups - 1, part, PART)
    split_rows(total, slice(0, width), sent, kept)


def stream_phase(ids, hidden, rank_down, weight):
    rows, depth = hidden.shape
    rank = rank_down.shape[0]
    width = weight.shape[1]
    return pl.pallas_call(
        stream_kernel,
        out_shape=(
            jax.ShapeDtypeStruct((rows, rank), jnp.float32),
            jax.ShapeDtypeStruct((rows // 2, width), jnp.bfloat16),
            jax.ShapeDtypeStruct((rows // 2, width), jnp.float32),
        ),
        in_specs=[HBM] * 4,
        out_specs=(VMEM,) * 3,
        scratch_shapes=[
            pltpu.VMEM(ids.shape, ids.dtype),
            pltpu.VMEM(hidden.shape, hidden.dtype),
            pltpu.VMEM(rank_down.shape, rank_down.dtype),
            pltpu.VMEM((rows, width), jnp.float32),
            pltpu.VMEM((SLOTS * GROUP * PART, width), weight.dtype),
            pltpu.SemaphoreType.DMA((3,)),
            pltpu.SemaphoreType.DMA((SLOTS * GROUP,)),
        ],
        compiler_params=pltpu.CompilerParams(vmem_limit_bytes=53 << 20),
        cost_estimate=pl.CostEstimate(
            flops=2 * rows * depth * (width + rank),
            bytes_accessed=2 * depth * (width + rank + rows),
            transcendentals=0,
        ),
        name="low_rank_and_base",
    )(ids, hidden, rank_down, weight)


def split_rows(total, at, sent, kept):
    block = total.shape[0] // 4
    bit = lax.rem(lax.axis_index("tp"), 2)
    for half in range(2):
        rows = pl.ds(half * block, block)
        there = pl.ds(pl.multiple_of((2 * half + 1 - bit) * block, block), block)
        here = pl.ds(pl.multiple_of((2 * half + bit) * block, block), block)
        sent[rows, at] = total[there, :].astype(sent.dtype)
        kept[rows, at] = total[here, :]


def join_kernel(ids, low, up_here, up_there, kept, got, residual, sent, total, joined):
    block = residual.shape[0]
    tp = lax.axis_index("tp")
    high, bit = lax.div(tp, 2), lax.rem(tp, 2)
    adapter = column_of(ids[...])
    here = jnp.where(adapter == tp.astype(jnp.float32), low[...], 0.0)
    there = jnp.where(adapter == (tp + 1 - 2 * bit).astype(jnp.float32), low[...], 0.0)
    halves = []
    for half in range(2):
        even = slice(2 * half * block, (2 * half + 1) * block)
        odd = slice((2 * half + 1) * block, (2 * half + 2) * block)
        halves.append([jnp.where(bit == 0, x[even], x[odd]) for x in (here, there)])
    coefficient = [
        jnp.concatenate([halves[0][i], halves[1][i]], axis=0).astype(jnp.bfloat16)
        for i in range(2)
    ]
    width = residual.shape[1]
    for start in range(0, width, TILE):
        at = slice(start, start + TILE)
        joined[:, at] = (
            kept[:, at]
            + got[:, at].astype(jnp.float32)
            + jnp.dot(coefficient[0], up_here[:, at], preferred_element_type=jnp.float32)
            + jnp.dot(coefficient[1], up_there[:, at], preferred_element_type=jnp.float32)
        )
    near = pl.ds(pl.multiple_of(high * block, block), block)
    far = pl.ds(pl.multiple_of((1 - high) * block, block), block)
    sent[...] = joined[far, :].astype(sent.dtype)
    total[...] = joined[near, :] + residual[...].astype(jnp.float32)


def join_phase(ids, low, up_here, up_there, kept, got, residual):
    return pl.pallas_call(
        join_kernel,
        out_shape=(
            jax.ShapeDtypeStruct(residual.shape, jnp.bfloat16),
            jax.ShapeDtypeStruct(residual.shape, jnp.float32),
        ),
        in_specs=[VMEM] * 7,
        out_specs=(VMEM,) * 2,
        scratch_shapes=[pltpu.VMEM(kept.shape, kept.dtype)],
        compiler_params=pltpu.CompilerParams(vmem_limit_bytes=8 << 20),
        name="join",
    )(ids, low, up_here, up_there, kept, got, residual)


def finish_kernel(total, got, mixed):
    mixed[...] = (total[...] + got[...].astype(jnp.float32)).astype(mixed.dtype)


def finish_phase(total, got):
    return pl.pallas_call(
        finish_kernel,
        out_shape=jax.ShapeDtypeStruct(total.shape, got.dtype),
        in_specs=[VMEM] * 2,
        out_specs=VMEM,
        compiler_params=pltpu.CompilerParams(vmem_limit_bytes=8 << 20),
        name="finish",
    )(total, got)


def swap(value, axis, bit=1):
    return lax.ppermute(value, axis, [(i, i ^ bit) for i in range(lax.axis_size(axis))])


def four_by_four(hidden, adapter_ids, weight, rank_down, rank_up, residual):
    ids = adapter_ids[None]
    up = rank_up[0]
    up_there = swap(up, "tp", 1)
    low, sent, kept = stream_phase(ids, hidden, jnp.swapaxes(rank_down, 1, 2)[0], weight)
    got = swap(sent, "tp", 1)
    low = low + swap(low, "sub")
    low = low + swap(low, "page")
    low = low + swap(low, "tp", 1)
    low = low + swap(low, "tp", 2)
    sent, total = join_phase(ids, low, up, up_there, kept, got, residual)
    return finish_phase(total, swap(sent, "tp", 2))


def any_size(hidden_units, adapter_ids, down_projection_weight, rank_down, rank_up, residual):
    owned_count = rank_down.shape[0]
    first_owned = lax.axis_index(PS) * owned_count
    chosen = (
        (adapter_ids - first_owned)[:, None] == jnp.arange(owned_count, dtype=jnp.int32)[None, :]
    ).astype(jnp.float32)
    projected = jnp.einsum(
        "rf,afk->rak", hidden_units, rank_down, preferred_element_type=jnp.float32
    )
    partial_low = jnp.einsum("rak,ra->rk", projected, chosen)
    low_rank = lax.psum(partial_low, ("tp",) + PS).astype(jnp.bfloat16)
    held_count, rank_width, columns = rank_up.shape
    first_held = lax.axis_index("tp") * held_count
    picked = (
        (adapter_ids - first_held)[:, None] == jnp.arange(held_count, dtype=jnp.int32)[None, :]
    ).astype(jnp.bfloat16)
    coefficient = (picked[:, :, None] * low_rank[:, None, :]).reshape(
        -1, held_count * rank_width
    )
    term = jnp.dot(
        hidden_units, down_projection_weight, preferred_element_type=jnp.float32
    ) + jnp.dot(
        coefficient,
        rank_up.reshape(held_count * rank_width, columns),
        preferred_element_type=jnp.float32,
    )
    summed = lax.psum_scatter(
        term.astype(jnp.bfloat16), "tp", scatter_dimension=0, tiled=True
    ).astype(jnp.float32)
    return (residual.astype(jnp.float32) + summed).astype(jnp.bfloat16)


def on_device(hidden_units, adapter_ids, down_projection_weight, rank_down, rank_up, residual):
    sizes = [lax.axis_size(axis) for axis in ("tp",) + PS]
    fits = (
        sizes[0] == 4
        and sizes[1] == 2
        and sizes[2] == 2
        and rank_down.shape[0] == 1
        and rank_up.shape[0] == 1
        and residual.shape == (16, 6 * TILE)
        and hidden_units.shape[1] % (GROUP * PART) == 0
        and hidden_units.shape[1] >= SLOTS * GROUP * PART
    )
    form = four_by_four if fits else any_size
    return form(hidden_units, adapter_ids, down_projection_weight, rank_down, rank_up, residual)


def solution(mesh):
    placed = (
        P("parts", "tp"),
        P("parts"),
        P("tp", ("page", "sub")),
        P(("parts", "page", "sub"), "tp", None),
        P(("parts", "tp"), None, ("page", "sub")),
        P(("parts", "tp"), ("page", "sub")),
    )
    return jax.shard_map(
        on_device,
        mesh=mesh,
        in_specs=placed,
        out_specs=P(("parts", "tp"), ("page", "sub")),
        check_vma=False,
    )
```

```python
import functools

import jax
import jax.numpy as jnp
from jax import lax
from jax.experimental import pallas as pl
from jax.experimental.pallas import tpu as pltpu
from jax.sharding import PartitionSpec as P

PART = 256
GROUP = 3
SLOTS = 6
TILE = 512
PS = ("page", "sub")
VMEM = pl.BlockSpec(memory_space=pltpu.VMEM)
HBM = pl.BlockSpec(memory_space=pltpu.HBM)


def column_of(ids_row):
    rows = ids_row.shape[1]
    down = lax.broadcasted_iota(jnp.int32, (rows, rows), 0)
    across = lax.broadcasted_iota(jnp.int32, (rows, rows), 1)
    spread = jnp.broadcast_to(ids_row, (rows, rows))
    return jnp.sum(
        jnp.where(down == across, spread.astype(jnp.float32), 0.0), axis=1, keepdims=True
    )


def stream_kernel(
    hidden, rank_down, weight, packed, sent, kept, hidden_here, down_here, total, held, got, arrived
):
    groups = weight.shape[0] // (PART * GROUP)
    width = weight.shape[1]
    deep = PART * GROUP

    def part_copy(group, part):
        rows = pl.ds(pl.multiple_of(group * deep + part * PART, PART), PART)
        slot = lax.rem(group, SLOTS)
        there = pl.ds(pl.multiple_of(slot * deep + part * PART, PART), PART)
        return pltpu.make_async_copy(
            weight.at[rows], held.at[there], arrived.at[slot * GROUP + part]
        )

    first = [
        pltpu.make_async_copy(hidden, hidden_here, got.at[0]),
        pltpu.make_async_copy(rank_down, down_here, got.at[1]),
    ]
    for copy in first:
        copy.start()

    @pl.loop(0, SLOTS - 1)
    def _(group):
        for part in range(GROUP):
            part_copy(group, part).start()

    total[...] = jnp.zeros_like(total)
    for copy in first:
        copy.wait()
    low = lax.dot_general(
        hidden_here[...],
        down_here[...],
        (((1,), (1,)), ((), ())),
        preferred_element_type=jnp.float32,
    )
    block = low.shape[0] // 4
    for bit in range(2):
        wanted = jnp.concatenate(
            [low[(half + bit) * block : (half + bit + 1) * block] for half in (0, 2)], axis=1
        )
        for to in range(packed.shape[0]):
            if (to // 4) % 2 == bit:
                packed[to] = wanted

    def add(group, part, depth):
        at = pl.ds(pl.multiple_of(group * deep + part * PART, PART), depth)
        slot = pl.ds(pl.multiple_of(lax.rem(group, SLOTS) * deep + part * PART, PART), depth)
        for start in range(0, width, TILE):
            columns = slice(start, start + TILE)
            total[:, columns] += jnp.dot(
                hidden_here[:, at], held[slot, columns], preferred_element_type=jnp.float32
            )

    @pl.loop(0, groups - 1)
    def _(group):
        @pl.when(group + SLOTS - 1 < groups)
        def _():
            for part in range(GROUP):
                part_copy(group + SLOTS - 1, part).start()

        for part in range(GROUP):
            part_copy(group, part).wait()
        add(group, 0, deep)

    for part in range(GROUP):
        part_copy(groups - 1, part).wait()
        add(groups - 1, part, PART)
    split_rows(total, slice(0, width), sent, kept)


def stream_phase(hidden, rank_down, weight):
    rows, depth = hidden.shape
    rank = rank_down.shape[0]
    width = weight.shape[1]
    return pl.pallas_call(
        stream_kernel,
        out_shape=(
            jax.ShapeDtypeStruct((16, rows // 4, 2 * rank), jnp.float32),
            jax.ShapeDtypeStruct((rows // 2, width), jnp.bfloat16),
            jax.ShapeDtypeStruct((rows // 2, width), jnp.float32),
        ),
        in_specs=[HBM] * 3,
        out_specs=(VMEM,) * 3,
        scratch_shapes=[
            pltpu.VMEM(hidden.shape, hidden.dtype),
            pltpu.VMEM(rank_down.shape, rank_down.dtype),
            pltpu.VMEM((rows, width), jnp.float32),
            pltpu.VMEM((SLOTS * GROUP * PART, width), weight.dtype),
            pltpu.SemaphoreType.DMA((2,)),
            pltpu.SemaphoreType.DMA((SLOTS * GROUP,)),
        ],
        compiler_params=pltpu.CompilerParams(vmem_limit_bytes=53 << 20),
        cost_estimate=pl.CostEstimate(
            flops=2 * rows * depth * (width + rank),
            bytes_accessed=2 * depth * (width + rank + rows),
            transcendentals=0,
        ),
        name="low_rank_and_base",
    )(hidden, rank_down, weight)


def split_rows(total, at, sent, kept):
    block = total.shape[0] // 4
    bit = lax.rem(lax.axis_index("tp"), 2)
    for half in range(2):
        rows = pl.ds(half * block, block)
        there = pl.ds(pl.multiple_of((2 * half + 1 - bit) * block, block), block)
        here = pl.ds(pl.multiple_of((2 * half + bit) * block, block), block)
        sent[rows, at] = total[there, :].astype(sent.dtype)
        kept[rows, at] = total[here, :]


def join_kernel(ids, packed, up_here, up_there, kept, got, residual, sent, total, joined):
    block = residual.shape[0]
    rank = up_here.shape[0]
    tp = lax.axis_index("tp")
    high, bit = lax.div(tp, 2), lax.rem(tp, 2)
    every = column_of(ids[...])
    parts = [every[index * block : (index + 1) * block] for index in range(4)]
    adapter = jnp.concatenate(
        [jnp.where(bit == 0, parts[half], parts[half + 1]) for half in (0, 2)], axis=0
    )
    coefficient = []
    for index in (tp, tp + 1 - 2 * bit):
        low = packed[index]
        for source in range(1, 4):
            low = low + packed[4 * source + index]
        low = jnp.concatenate([low[:, :rank], low[:, rank:]], axis=0)
        low = jnp.where(adapter == index.astype(jnp.float32), low, 0.0)
        coefficient.append(low.astype(jnp.bfloat16))
    width = residual.shape[1]
    for start in range(0, width, TILE):
        at = slice(start, start + TILE)
        joined[:, at] = (
            kept[:, at]
            + got[:, at].astype(jnp.float32)
            + jnp.dot(coefficient[0], up_here[:, at], preferred_element_type=jnp.float32)
            + jnp.dot(coefficient[1], up_there[:, at], preferred_element_type=jnp.float32)
        )
    near = pl.ds(pl.multiple_of(high * block, block), block)
    far = pl.ds(pl.multiple_of((1 - high) * block, block), block)
    sent[...] = joined[far, :].astype(sent.dtype)
    total[...] = joined[near, :] + residual[...].astype(jnp.float32)


def join_phase(ids, packed, up_here, up_there, kept, got, residual):
    return pl.pallas_call(
        join_kernel,
        out_shape=(
            jax.ShapeDtypeStruct(residual.shape, jnp.bfloat16),
            jax.ShapeDtypeStruct(residual.shape, jnp.float32),
        ),
        in_specs=[VMEM] * 7,
        out_specs=(VMEM,) * 2,
        scratch_shapes=[pltpu.VMEM(kept.shape, kept.dtype)],
        compiler_params=pltpu.CompilerParams(vmem_limit_bytes=8 << 20),
        name="join",
    )(ids, packed, up_here, up_there, kept, got, residual)


def finish_kernel(total, got, mixed):
    mixed[...] = (total[...] + got[...].astype(jnp.float32)).astype(mixed.dtype)


def finish_phase(total, got):
    return pl.pallas_call(
        finish_kernel,
        out_shape=jax.ShapeDtypeStruct(total.shape, got.dtype),
        in_specs=[VMEM] * 2,
        out_specs=VMEM,
        compiler_params=pltpu.CompilerParams(vmem_limit_bytes=8 << 20),
        name="finish",
    )(total, got)


def swap(value, bit):
    return lax.ppermute(value, "tp", [(i, i ^ bit) for i in range(lax.axis_size("tp"))])


def four_by_four(hidden, adapter_ids, weight, rank_down, rank_up, residual):
    up = rank_up[0]
    up_there = swap(up, 1)
    packed, sent, kept = stream_phase(hidden, jnp.swapaxes(rank_down, 1, 2)[0], weight)
    got = swap(sent, 1)
    packed = lax.all_to_all(packed, ("tp",) + PS, split_axis=0, concat_axis=0, tiled=True)
    sent, total = join_phase(adapter_ids[None], packed, up, up_there, kept, got, residual)
    return finish_phase(total, swap(sent, 2))


def any_size(hidden_units, adapter_ids, down_projection_weight, rank_down, rank_up, residual):
    owned_count = rank_down.shape[0]
    first_owned = lax.axis_index(PS) * owned_count
    chosen = (
        (adapter_ids - first_owned)[:, None] == jnp.arange(owned_count, dtype=jnp.int32)[None, :]
    ).astype(jnp.float32)
    projected = jnp.einsum(
        "rf,afk->rak", hidden_units, rank_down, preferred_element_type=jnp.float32
    )
    partial_low = jnp.einsum("rak,ra->rk", projected, chosen)
    low_rank = lax.psum(partial_low, ("tp",) + PS).astype(jnp.bfloat16)
    held_count, rank_width, columns = rank_up.shape
    first_held = lax.axis_index("tp") * held_count
    picked = (
        (adapter_ids - first_held)[:, None] == jnp.arange(held_count, dtype=jnp.int32)[None, :]
    ).astype(jnp.bfloat16)
    coefficient = (picked[:, :, None] * low_rank[:, None, :]).reshape(
        -1, held_count * rank_width
    )
    term = jnp.dot(
        hidden_units, down_projection_weight, preferred_element_type=jnp.float32
    ) + jnp.dot(
        coefficient,
        rank_up.reshape(held_count * rank_width, columns),
        preferred_element_type=jnp.float32,
    )
    summed = lax.psum_scatter(
        term.astype(jnp.bfloat16), "tp", scatter_dimension=0, tiled=True
    ).astype(jnp.float32)
    return (residual.astype(jnp.float32) + summed).astype(jnp.bfloat16)


def on_device(hidden_units, adapter_ids, down_projection_weight, rank_down, rank_up, residual):
    sizes = [lax.axis_size(axis) for axis in ("tp",) + PS]
    fits = (
        sizes[0] == 4
        and sizes[1] == 2
        and sizes[2] == 2
        and rank_down.shape[0] == 1
        and rank_up.shape[0] == 1
        and residual.shape == (16, 6 * TILE)
        and hidden_units.shape[1] % (GROUP * PART) == 0
        and hidden_units.shape[1] >= SLOTS * GROUP * PART
    )
    form = four_by_four if fits else any_size
    return form(hidden_units, adapter_ids, down_projection_weight, rank_down, rank_up, residual)


def solution(mesh):
    placed = (
        P("parts", "tp"),
        P("parts"),
        P("tp", ("page", "sub")),
        P(("parts", "page", "sub"), "tp", None),
        P(("parts", "tp"), None, ("page", "sub")),
        P(("parts", "tp"), ("page", "sub")),
    )
    return jax.shard_map(
        on_device,
        mesh=mesh,
        in_specs=placed,
        out_specs=P(("parts", "tp"), ("page", "sub")),
        check_vma=False,
    )
```

```python
import functools

import jax
import jax.numpy as jnp
from jax import lax
from jax.experimental import pallas as pl
from jax.experimental.pallas import tpu as pltpu
from jax.sharding import PartitionSpec as P

PART = 256
GROUP = 3
SLOTS = 6
TILE = 512
PS = ("page", "sub")
VMEM = pl.BlockSpec(memory_space=pltpu.VMEM)
HBM = pl.BlockSpec(memory_space=pltpu.HBM)


def column_of(ids_row):
    rows = ids_row.shape[1]
    down = lax.broadcasted_iota(jnp.int32, (rows, rows), 0)
    across = lax.broadcasted_iota(jnp.int32, (rows, rows), 1)
    spread = jnp.broadcast_to(ids_row, (rows, rows))
    return jnp.sum(
        jnp.where(down == across, spread.astype(jnp.float32), 0.0), axis=1, keepdims=True
    )


def stream_kernel(
    hidden, rank_down, weight, packed, sent, kept, hidden_here, down_here, total, held, got, arrived
):
    groups = weight.shape[0] // (PART * GROUP)
    width = weight.shape[1]
    deep = PART * GROUP

    def part_copy(group, part):
        rows = pl.ds(pl.multiple_of(group * deep + part * PART, PART), PART)
        slot = lax.rem(group, SLOTS)
        there = pl.ds(pl.multiple_of(slot * deep + part * PART, PART), PART)
        return pltpu.make_async_copy(
            weight.at[rows], held.at[there], arrived.at[slot * GROUP + part]
        )

    first = [
        pltpu.make_async_copy(hidden, hidden_here, got.at[0]),
        pltpu.make_async_copy(rank_down, down_here, got.at[1]),
    ]
    for copy in first:
        copy.start()

    @pl.loop(0, SLOTS - 1)
    def _(group):
        for part in range(GROUP):
            part_copy(group, part).start()

    total[...] = jnp.zeros_like(total)
    for copy in first:
        copy.wait()
    low = lax.dot_general(
        hidden_here[...],
        down_here[...],
        (((1,), (1,)), ((), ())),
        preferred_element_type=jnp.float32,
    )
    block = low.shape[0] // 4
    for bit in range(2):
        wanted = jnp.concatenate(
            [low[(half + bit) * block : (half + bit + 1) * block] for half in (0, 2)], axis=1
        )
        for to in range(packed.shape[0]):
            if (to // 4) % 2 == bit:
                packed[to] = wanted

    def add(group, part, depth):
        at = pl.ds(pl.multiple_of(group * deep + part * PART, PART), depth)
        slot = pl.ds(pl.multiple_of(lax.rem(group, SLOTS) * deep + part * PART, PART), depth)
        for start in range(0, width, TILE):
            columns = slice(start, start + TILE)
            total[:, columns] += jnp.dot(
                hidden_here[:, at], held[slot, columns], preferred_element_type=jnp.float32
            )

    @pl.loop(0, groups - 1)
    def _(group):
        @pl.when(group + SLOTS - 1 < groups)
        def _():
            for part in range(GROUP):
                part_copy(group + SLOTS - 1, part).start()

        for part in range(GROUP):
            part_copy(group, part).wait()
        add(group, 0, deep)

    for part in range(GROUP):
        part_copy(groups - 1, part).wait()
        add(groups - 1, part, PART)
    split_rows(total, slice(0, width), sent, kept)


def stream_phase(hidden, rank_down, weight):
    rows, depth = hidden.shape
    rank = rank_down.shape[0]
    width = weight.shape[1]
    return pl.pallas_call(
        stream_kernel,
        out_shape=(
            jax.ShapeDtypeStruct((16, rows // 4, 2 * rank), jnp.float32),
            jax.ShapeDtypeStruct((rows // 2, width), jnp.bfloat16),
            jax.ShapeDtypeStruct((rows // 2, width), jnp.float32),
        ),
        in_specs=[HBM] * 3,
        out_specs=(VMEM,) * 3,
        scratch_shapes=[
            pltpu.VMEM(hidden.shape, hidden.dtype),
            pltpu.VMEM(rank_down.shape, rank_down.dtype),
            pltpu.VMEM((rows, width), jnp.float32),
            pltpu.VMEM((SLOTS * GROUP * PART, width), weight.dtype),
            pltpu.SemaphoreType.DMA((2,)),
            pltpu.SemaphoreType.DMA((SLOTS * GROUP,)),
        ],
        compiler_params=pltpu.CompilerParams(vmem_limit_bytes=53 << 20),
        cost_estimate=pl.CostEstimate(
            flops=2 * rows * depth * (width + rank),
            bytes_accessed=2 * depth * (width + rank + rows),
            transcendentals=0,
        ),
        name="low_rank_and_base",
    )(hidden, rank_down, weight)


def split_rows(total, at, sent, kept):
    block = total.shape[0] // 4
    bit = lax.rem(lax.axis_index("tp"), 2)
    for half in range(2):
        rows = pl.ds(half * block, block)
        there = pl.ds(pl.multiple_of((2 * half + 1 - bit) * block, block), block)
        here = pl.ds(pl.multiple_of((2 * half + bit) * block, block), block)
        sent[rows, at] = total[there, :].astype(sent.dtype)
        kept[rows, at] = total[here, :]


def pair_kernel(kept, got, pair):
    pair[...] = kept[...] + got[...].astype(jnp.float32)


def pair_phase(kept, got):
    return pl.pallas_call(
        pair_kernel,
        out_shape=jax.ShapeDtypeStruct(kept.shape, kept.dtype),
        in_specs=[VMEM] * 2,
        out_specs=VMEM,
        compiler_params=pltpu.CompilerParams(vmem_limit_bytes=8 << 20),
        cost_estimate=pl.CostEstimate(flops=1 << 34, bytes_accessed=1 << 28, transcendentals=0),
        name="pair_sum",
    )(kept, got)


def join_kernel(ids, packed, up_here, up_there, pair, residual, sent, total, joined):
    block = residual.shape[0]
    rank = up_here.shape[0]
    tp = lax.axis_index("tp")
    high, bit = lax.div(tp, 2), lax.rem(tp, 2)
    every = column_of(ids[...])
    parts = [every[index * block : (index + 1) * block] for index in range(4)]
    adapter = jnp.concatenate(
        [jnp.where(bit == 0, parts[half], parts[half + 1]) for half in (0, 2)], axis=0
    )
    coefficient = []
    for index in (tp, tp + 1 - 2 * bit):
        low = packed[index]
        for source in range(1, 4):
            low = low + packed[4 * source + index]
        low = jnp.concatenate([low[:, :rank], low[:, rank:]], axis=0)
        low = jnp.where(adapter == index.astype(jnp.float32), low, 0.0)
        coefficient.append(low.astype(jnp.bfloat16))
    width = residual.shape[1]
    for start in range(0, width, TILE):
        at = slice(start, start + TILE)
        joined[:, at] = (
            pair[:, at]
            + jnp.dot(coefficient[0], up_here[:, at], preferred_element_type=jnp.float32)
            + jnp.dot(coefficient[1], up_there[:, at], preferred_element_type=jnp.float32)
        )
    near = pl.ds(pl.multiple_of(high * block, block), block)
    far = pl.ds(pl.multiple_of((1 - high) * block, block), block)
    sent[...] = joined[far, :].astype(sent.dtype)
    total[...] = joined[near, :] + residual[...].astype(jnp.float32)


def join_phase(ids, packed, up_here, up_there, pair, residual):
    return pl.pallas_call(
        join_kernel,
        out_shape=(
            jax.ShapeDtypeStruct(residual.shape, jnp.bfloat16),
            jax.ShapeDtypeStruct(residual.shape, jnp.float32),
        ),
        in_specs=[VMEM] * 6,
        out_specs=(VMEM,) * 2,
        scratch_shapes=[pltpu.VMEM(pair.shape, pair.dtype)],
        compiler_params=pltpu.CompilerParams(vmem_limit_bytes=8 << 20),
        name="join",
    )(ids, packed, up_here, up_there, pair, residual)


def finish_kernel(total, got, mixed):
    mixed[...] = (total[...] + got[...].astype(jnp.float32)).astype(mixed.dtype)


def finish_phase(total, got):
    return pl.pallas_call(
        finish_kernel,
        out_shape=jax.ShapeDtypeStruct(total.shape, got.dtype),
        in_specs=[VMEM] * 2,
        out_specs=VMEM,
        compiler_params=pltpu.CompilerParams(vmem_limit_bytes=8 << 20),
        name="finish",
    )(total, got)


def swap(value, bit):
    return lax.ppermute(value, "tp", [(i, i ^ bit) for i in range(lax.axis_size("tp"))])


def four_by_four(hidden, adapter_ids, weight, rank_down, rank_up, residual):
    up = rank_up[0]
    up_there = swap(up, 1)
    packed, sent, kept = stream_phase(hidden, jnp.swapaxes(rank_down, 1, 2)[0], weight)
    pair = pair_phase(kept, swap(sent, 1))
    packed = lax.all_to_all(packed, ("tp",) + PS, split_axis=0, concat_axis=0, tiled=True)
    sent, total = join_phase(adapter_ids[None], packed, up, up_there, pair, residual)
    return finish_phase(total, swap(sent, 2))


def any_size(hidden_units, adapter_ids, down_projection_weight, rank_down, rank_up, residual):
    owned_count = rank_down.shape[0]
    first_owned = lax.axis_index(PS) * owned_count
    chosen = (
        (adapter_ids - first_owned)[:, None] == jnp.arange(owned_count, dtype=jnp.int32)[None, :]
    ).astype(jnp.float32)
    projected = jnp.einsum(
        "rf,afk->rak", hidden_units, rank_down, preferred_element_type=jnp.float32
    )
    partial_low = jnp.einsum("rak,ra->rk", projected, chosen)
    low_rank = lax.psum(partial_low, ("tp",) + PS).astype(jnp.bfloat16)
    held_count, rank_width, columns = rank_up.shape
    first_held = lax.axis_index("tp") * held_count
    picked = (
        (adapter_ids - first_held)[:, None] == jnp.arange(held_count, dtype=jnp.int32)[None, :]
    ).astype(jnp.bfloat16)
    coefficient = (picked[:, :, None] * low_rank[:, None, :]).reshape(
        -1, held_count * rank_width
    )
    term = jnp.dot(
        hidden_units, down_projection_weight, preferred_element_type=jnp.float32
    ) + jnp.dot(
        coefficient,
        rank_up.reshape(held_count * rank_width, columns),
        preferred_element_type=jnp.float32,
    )
    summed = lax.psum_scatter(
        term.astype(jnp.bfloat16), "tp", scatter_dimension=0, tiled=True
    ).astype(jnp.float32)
    return (residual.astype(jnp.float32) + summed).astype(jnp.bfloat16)


def on_device(hidden_units, adapter_ids, down_projection_weight, rank_down, rank_up, residual):
    sizes = [lax.axis_size(axis) for axis in ("tp",) + PS]
    fits = (
        sizes[0] == 4
        and sizes[1] == 2
        and sizes[2] == 2
        and rank_down.shape[0] == 1
        and rank_up.shape[0] == 1
        and residual.shape == (16, 6 * TILE)
        and hidden_units.shape[1] % (GROUP * PART) == 0
        and hidden_units.shape[1] >= SLOTS * GROUP * PART
    )
    form = four_by_four if fits else any_size
    return form(hidden_units, adapter_ids, down_projection_weight, rank_down, rank_up, residual)


def solution(mesh):
    placed = (
        P("parts", "tp"),
        P("parts"),
        P("tp", ("page", "sub")),
        P(("parts", "page", "sub"), "tp", None),
        P(("parts", "tp"), None, ("page", "sub")),
        P(("parts", "tp"), ("page", "sub")),
    )
    return jax.shard_map(
        on_device,
        mesh=mesh,
        in_specs=placed,
        out_specs=P(("parts", "tp"), ("page", "sub")),
        check_vma=False,
    )
```

```python
import functools

import jax
import jax.numpy as jnp
from jax import lax
from jax.experimental import pallas as pl
from jax.experimental.pallas import tpu as pltpu
from jax.sharding import PartitionSpec as P

PART = 256
GROUP = 3
SLOTS = 6
TILE = 512
PS = ("page", "sub")
VMEM = pl.BlockSpec(memory_space=pltpu.VMEM)
HBM = pl.BlockSpec(memory_space=pltpu.HBM)


def column_of(ids_row):
    rows = ids_row.shape[1]
    down = lax.broadcasted_iota(jnp.int32, (rows, rows), 0)
    across = lax.broadcasted_iota(jnp.int32, (rows, rows), 1)
    spread = jnp.broadcast_to(ids_row, (rows, rows))
    return jnp.sum(
        jnp.where(down == across, spread.astype(jnp.float32), 0.0), axis=1, keepdims=True
    )


def stream_kernel(
    hidden, rank_down, weight, packed, sent, kept, hidden_here, down_here, total, held, got, arrived
):
    groups = weight.shape[0] // (PART * GROUP)
    width = weight.shape[1]
    deep = PART * GROUP

    def part_copy(group, part):
        rows = pl.ds(pl.multiple_of(group * deep + part * PART, PART), PART)
        slot = lax.rem(group, SLOTS)
        there = pl.ds(pl.multiple_of(slot * deep + part * PART, PART), PART)
        return pltpu.make_async_copy(
            weight.at[rows], held.at[there], arrived.at[slot * GROUP + part]
        )

    first = [
        pltpu.make_async_copy(hidden, hidden_here, got.at[0]),
        pltpu.make_async_copy(rank_down, down_here, got.at[1]),
    ]
    for copy in first:
        copy.start()

    @pl.loop(0, SLOTS - 1)
    def _(group):
        for part in range(GROUP):
            part_copy(group, part).start()

    total[...] = jnp.zeros_like(total)
    for copy in first:
        copy.wait()
    low = lax.dot_general(
        hidden_here[...],
        down_here[...],
        (((1,), (1,)), ((), ())),
        preferred_element_type=jnp.float32,
    )
    block = low.shape[0] // 4
    for bit in range(2):
        wanted = jnp.concatenate(
            [low[(half + bit) * block : (half + bit + 1) * block] for half in (0, 2)], axis=1
        )
        for to in range(packed.shape[0]):
            if (to // 4) % 2 == bit:
                packed[to] = wanted

    def add(group, part, depth):
        at = pl.ds(pl.multiple_of(group * deep + part * PART, PART), depth)
        slot = pl.ds(pl.multiple_of(lax.rem(group, SLOTS) * deep + part * PART, PART), depth)
        for start in range(0, width, TILE):
            columns = slice(start, start + TILE)
            total[:, columns] += jnp.dot(
                hidden_here[:, at], held[slot, columns], preferred_element_type=jnp.float32
            )

    @pl.loop(0, groups - 1)
    def _(group):
        @pl.when(group + SLOTS - 1 < groups)
        def _():
            for part in range(GROUP):
                part_copy(group + SLOTS - 1, part).start()

        for part in range(GROUP):
            part_copy(group, part).wait()
        add(group, 0, deep)

    for part in range(GROUP):
        part_copy(groups - 1, part).wait()
        add(groups - 1, part, PART)
    split_rows(total, slice(0, width), sent, kept)


def stream_phase(hidden, rank_down, weight):
    rows, depth = hidden.shape
    rank = rank_down.shape[0]
    width = weight.shape[1]
    return pl.pallas_call(
        stream_kernel,
        out_shape=(
            jax.ShapeDtypeStruct((16, rows // 4, 2 * rank), jnp.float32),
            jax.ShapeDtypeStruct((rows // 2, width), jnp.bfloat16),
            jax.ShapeDtypeStruct((rows // 2, width), jnp.float32),
        ),
        in_specs=[HBM] * 3,
        out_specs=(VMEM,) * 3,
        scratch_shapes=[
            pltpu.VMEM(hidden.shape, hidden.dtype),
            pltpu.VMEM(rank_down.shape, rank_down.dtype),
            pltpu.VMEM((rows, width), jnp.float32),
            pltpu.VMEM((SLOTS * GROUP * PART, width), weight.dtype),
            pltpu.SemaphoreType.DMA((2,)),
            pltpu.SemaphoreType.DMA((SLOTS * GROUP,)),
        ],
        compiler_params=pltpu.CompilerParams(vmem_limit_bytes=53 << 20),
        cost_estimate=pl.CostEstimate(
            flops=2 * rows * depth * (width + rank),
            bytes_accessed=2 * depth * (width + rank + rows),
            transcendentals=0,
        ),
        name="low_rank_and_base",
    )(hidden, rank_down, weight)


def split_rows(total, at, sent, kept):
    block = total.shape[0] // 4
    bit = lax.rem(lax.axis_index("tp"), 2)
    for half in range(2):
        rows = pl.ds(half * block, block)
        there = pl.ds(pl.multiple_of((2 * half + 1 - bit) * block, block), block)
        here = pl.ds(pl.multiple_of((2 * half + bit) * block, block), block)
        sent[rows, at] = total[there, :].astype(sent.dtype)
        kept[rows, at] = total[here, :]


def pair_kernel(kept, got, pair):
    pair[...] = kept[...] + got[...].astype(jnp.float32)


def pair_phase(kept, got):
    return pl.pallas_call(
        pair_kernel,
        out_shape=jax.ShapeDtypeStruct(kept.shape, kept.dtype),
        in_specs=[VMEM] * 2,
        out_specs=VMEM,
        compiler_params=pltpu.CompilerParams(vmem_limit_bytes=8 << 20),
        cost_estimate=pl.CostEstimate(flops=1 << 34, bytes_accessed=1 << 28, transcendentals=0),
        name="pair_sum",
    )(kept, got)


def join_kernel(ids, packed, up_here, up_there, pair, residual, sent, total, joined):
    block = residual.shape[0]
    rank = up_here.shape[0]
    tp = lax.axis_index("tp")
    high, bit = lax.div(tp, 2), lax.rem(tp, 2)
    every = column_of(ids[...])
    parts = [every[index * block : (index + 1) * block] for index in range(4)]
    adapter = jnp.concatenate(
        [jnp.where(bit == 0, parts[half], parts[half + 1]) for half in (0, 2)], axis=0
    )
    coefficient = []
    for index in (tp, tp + 1 - 2 * bit):
        low = packed[index]
        for source in range(1, 4):
            low = low + packed[4 * source + index]
        low = jnp.concatenate([low[:, :rank], low[:, rank:]], axis=0)
        low = jnp.where(adapter == index.astype(jnp.float32), low, 0.0)
        coefficient.append(low.astype(jnp.bfloat16))
    width = residual.shape[1]
    for start in range(0, width, TILE):
        at = slice(start, start + TILE)
        joined[:, at] = (
            pair[:, at]
            + jnp.dot(coefficient[0], up_here[:, at], preferred_element_type=jnp.float32)
            + jnp.dot(coefficient[1], up_there[:, at], preferred_element_type=jnp.float32)
        )
    near = pl.ds(pl.multiple_of(high * block, block), block)
    far = pl.ds(pl.multiple_of((1 - high) * block, block), block)
    sent[...] = joined[far, :].astype(sent.dtype)
    total[...] = joined[near, :] + residual[...].astype(jnp.float32)


def join_phase(ids, packed, up_here, up_there, pair, residual):
    return pl.pallas_call(
        join_kernel,
        out_shape=(
            jax.ShapeDtypeStruct(residual.shape, jnp.bfloat16),
            jax.ShapeDtypeStruct(residual.shape, jnp.float32),
        ),
        in_specs=[VMEM] * 6,
        out_specs=(VMEM,) * 2,
        scratch_shapes=[pltpu.VMEM(pair.shape, pair.dtype)],
        compiler_params=pltpu.CompilerParams(vmem_limit_bytes=8 << 20),
        name="join",
    )(ids, packed, up_here, up_there, pair, residual)


def finish_kernel(total, got, mixed):
    mixed[...] = (total[...] + got[...].astype(jnp.float32)).astype(mixed.dtype)


def finish_phase(total, got):
    return pl.pallas_call(
        finish_kernel,
        out_shape=jax.ShapeDtypeStruct(total.shape, got.dtype),
        in_specs=[VMEM] * 2,
        out_specs=VMEM,
        compiler_params=pltpu.CompilerParams(vmem_limit_bytes=8 << 20),
        name="finish",
    )(total, got)


def swap(value, bit):
    return lax.ppermute(value, "tp", [(i, i ^ bit) for i in range(lax.axis_size("tp"))])


def four_by_four(hidden, adapter_ids, weight, rank_down, rank_up, residual):
    up = rank_up[0]
    up_there = swap(up, 1)
    packed, sent, kept = stream_phase(hidden, jnp.swapaxes(rank_down, 1, 2)[0], weight)
    sent, up_there = lax.optimization_barrier((sent, up_there))
    pair = pair_phase(kept, swap(sent, 1))
    packed = lax.all_to_all(packed, ("tp",) + PS, split_axis=0, concat_axis=0, tiled=True)
    sent, total = join_phase(adapter_ids[None], packed, up, up_there, pair, residual)
    return finish_phase(total, swap(sent, 2))


def any_size(hidden_units, adapter_ids, down_projection_weight, rank_down, rank_up, residual):
    owned_count = rank_down.shape[0]
    first_owned = lax.axis_index(PS) * owned_count
    chosen = (
        (adapter_ids - first_owned)[:, None] == jnp.arange(owned_count, dtype=jnp.int32)[None, :]
    ).astype(jnp.float32)
    projected = jnp.einsum(
        "rf,afk->rak", hidden_units, rank_down, preferred_element_type=jnp.float32
    )
    partial_low = jnp.einsum("rak,ra->rk", projected, chosen)
    low_rank = lax.psum(partial_low, ("tp",) + PS).astype(jnp.bfloat16)
    held_count, rank_width, columns = rank_up.shape
    first_held = lax.axis_index("tp") * held_count
    picked = (
        (adapter_ids - first_held)[:, None] == jnp.arange(held_count, dtype=jnp.int32)[None, :]
    ).astype(jnp.bfloat16)
    coefficient = (picked[:, :, None] * low_rank[:, None, :]).reshape(
        -1, held_count * rank_width
    )
    term = jnp.dot(
        hidden_units, down_projection_weight, preferred_element_type=jnp.float32
    ) + jnp.dot(
        coefficient,
        rank_up.reshape(held_count * rank_width, columns),
        preferred_element_type=jnp.float32,
    )
    summed = lax.psum_scatter(
        term.astype(jnp.bfloat16), "tp", scatter_dimension=0, tiled=True
    ).astype(jnp.float32)
    return (residual.astype(jnp.float32) + summed).astype(jnp.bfloat16)


def on_device(hidden_units, adapter_ids, down_projection_weight, rank_down, rank_up, residual):
    sizes = [lax.axis_size(axis) for axis in ("tp",) + PS]
    fits = (
        sizes[0] == 4
        and sizes[1] == 2
        and sizes[2] == 2
        and rank_down.shape[0] == 1
        and rank_up.shape[0] == 1
        and residual.shape == (16, 6 * TILE)
        and hidden_units.shape[1] % (GROUP * PART) == 0
        and hidden_units.shape[1] >= SLOTS * GROUP * PART
    )
    form = four_by_four if fits else any_size
    return form(hidden_units, adapter_ids, down_projection_weight, rank_down, rank_up, residual)


def solution(mesh):
    placed = (
        P("parts", "tp"),
        P("parts"),
        P("tp", ("page", "sub")),
        P(("parts", "page", "sub"), "tp", None),
        P(("parts", "tp"), None, ("page", "sub")),
        P(("parts", "tp"), ("page", "sub")),
    )
    return jax.shard_map(
        on_device,
        mesh=mesh,
        in_specs=placed,
        out_specs=P(("parts", "tp"), ("page", "sub")),
        check_vma=False,
    )
```

```python
import functools

import jax
import jax.numpy as jnp
from jax import lax
from jax.experimental import pallas as pl
from jax.experimental.pallas import tpu as pltpu
from jax.sharding import PartitionSpec as P

PART = 256
GROUP = 3
SLOTS = 6
TILE = 512
PS = ("page", "sub")
VMEM = pl.BlockSpec(memory_space=pltpu.VMEM)
HBM = pl.BlockSpec(memory_space=pltpu.HBM)


def column_of(ids_row):
    rows = ids_row.shape[1]
    down = lax.broadcasted_iota(jnp.int32, (rows, rows), 0)
    across = lax.broadcasted_iota(jnp.int32, (rows, rows), 1)
    spread = jnp.broadcast_to(ids_row, (rows, rows))
    return jnp.sum(
        jnp.where(down == across, spread.astype(jnp.float32), 0.0), axis=1, keepdims=True
    )


def stream_kernel(
    hidden, rank_down, weight, packed, sent, kept, hidden_here, down_here, total, held, got, arrived
):
    groups = weight.shape[0] // (PART * GROUP)
    width = weight.shape[1]
    deep = PART * GROUP

    def part_copy(group, part):
        rows = pl.ds(pl.multiple_of(group * deep + part * PART, PART), PART)
        slot = lax.rem(group, SLOTS)
        there = pl.ds(pl.multiple_of(slot * deep + part * PART, PART), PART)
        return pltpu.make_async_copy(
            weight.at[rows], held.at[there], arrived.at[slot * GROUP + part]
        )

    first = [
        pltpu.make_async_copy(hidden, hidden_here, got.at[0]),
        pltpu.make_async_copy(rank_down, down_here, got.at[1]),
    ]
    for copy in first:
        copy.start()

    @pl.loop(0, SLOTS - 1)
    def _(group):
        for part in range(GROUP):
            part_copy(group, part).start()

    total[...] = jnp.zeros_like(total)
    for copy in first:
        copy.wait()
    low = lax.dot_general(
        hidden_here[...],
        down_here[...],
        (((1,), (1,)), ((), ())),
        preferred_element_type=jnp.float32,
    )
    half = low.shape[0] // 2
    packed[...] = jnp.concatenate([low[:half], low[half:]], axis=1)

    def add(group, part, depth):
        at = pl.ds(pl.multiple_of(group * deep + part * PART, PART), depth)
        slot = pl.ds(pl.multiple_of(lax.rem(group, SLOTS) * deep + part * PART, PART), depth)
        for start in range(0, width, TILE):
            columns = slice(start, start + TILE)
            total[:, columns] += jnp.dot(
                hidden_here[:, at], held[slot, columns], preferred_element_type=jnp.float32
            )

    @pl.loop(0, groups - 1)
    def _(group):
        @pl.when(group + SLOTS - 1 < groups)
        def _():
            for part in range(GROUP):
                part_copy(group + SLOTS - 1, part).start()

        for part in range(GROUP):
            part_copy(group, part).wait()
        add(group, 0, deep)

    for part in range(GROUP):
        part_copy(groups - 1, part).wait()
        add(groups - 1, part, PART)
    split_rows(total, slice(0, width), sent, kept)


def stream_phase(hidden, rank_down, weight):
    rows, depth = hidden.shape
    rank = rank_down.shape[0]
    width = weight.shape[1]
    return pl.pallas_call(
        stream_kernel,
        out_shape=(
            jax.ShapeDtypeStruct((rows // 2, 2 * rank), jnp.float32),
            jax.ShapeDtypeStruct((rows // 2, width), jnp.bfloat16),
            jax.ShapeDtypeStruct((rows // 2, width), jnp.float32),
        ),
        in_specs=[HBM] * 3,
        out_specs=(VMEM,) * 3,
        scratch_shapes=[
            pltpu.VMEM(hidden.shape, hidden.dtype),
            pltpu.VMEM(rank_down.shape, rank_down.dtype),
            pltpu.VMEM((rows, width), jnp.float32),
            pltpu.VMEM((SLOTS * GROUP * PART, width), weight.dtype),
            pltpu.SemaphoreType.DMA((2,)),
            pltpu.SemaphoreType.DMA((SLOTS * GROUP,)),
        ],
        compiler_params=pltpu.CompilerParams(vmem_limit_bytes=53 << 20),
        cost_estimate=pl.CostEstimate(
            flops=2 * rows * depth * (width + rank),
            bytes_accessed=2 * depth * (width + rank + rows),
            transcendentals=0,
        ),
        name="low_rank_and_base",
    )(hidden, rank_down, weight)


def split_rows(total, at, sent, kept):
    block = total.shape[0] // 4
    bit = lax.rem(lax.axis_index("tp"), 2)
    for half in range(2):
        rows = pl.ds(half * block, block)
        there = pl.ds(pl.multiple_of((2 * half + 1 - bit) * block, block), block)
        here = pl.ds(pl.multiple_of((2 * half + bit) * block, block), block)
        sent[rows, at] = total[there, :].astype(sent.dtype)
        kept[rows, at] = total[here, :]


def unpacked(packed):
    rank = packed.shape[1] // 2
    return jnp.concatenate([packed[:, :rank], packed[:, rank:]], axis=0)


def merge_kernel(ids, own, other, same, flipped):
    page, sub = lax.axis_index("page"), lax.axis_index("sub")
    adapter = column_of(ids[...])
    mine = (2 * page + sub).astype(jnp.float32)
    theirs = (2 * page + 1 - sub).astype(jnp.float32)
    low = jnp.where(
        adapter == mine,
        unpacked(own[...]),
        jnp.where(adapter == theirs, unpacked(other[...]), 0.0),
    )
    block = low.shape[0] // 4
    rows = [low[index * block : (index + 1) * block] for index in range(4)]
    even = jnp.concatenate([rows[0], rows[2]], axis=1)
    odd = jnp.concatenate([rows[1], rows[3]], axis=1)
    bit = lax.rem(lax.axis_index("tp"), 2)
    same[...] = jnp.where(bit == 0, even, odd)
    flipped[...] = jnp.where(bit == 0, odd, even)


def merge_phase(ids, own, other):
    shape = jax.ShapeDtypeStruct((own.shape[0] // 2, own.shape[1]), own.dtype)
    return pl.pallas_call(
        merge_kernel,
        out_shape=(shape, shape),
        in_specs=[VMEM] * 3,
        out_specs=(VMEM,) * 2,
        compiler_params=pltpu.CompilerParams(vmem_limit_bytes=4 << 20),
        name="merge_low_rank",
    )(ids, own, other)


def join_kernel(ids, near, far, up_here, up_there, kept, got, residual, sent, total, joined):
    block = residual.shape[0]
    tp = lax.axis_index("tp")
    high, bit = lax.div(tp, 2), lax.rem(tp, 2)
    every = column_of(ids[...])
    parts = [every[index * block : (index + 1) * block] for index in range(4)]
    adapter = jnp.concatenate(
        [jnp.where(bit == 0, parts[half], parts[half + 1]) for half in (0, 2)], axis=0
    )
    low = unpacked(near[...] + far[...])
    coefficient = [
        jnp.where(adapter == index.astype(jnp.float32), low, 0.0).astype(jnp.bfloat16)
        for index in (tp, tp + 1 - 2 * bit)
    ]
    width = residual.shape[1]
    for start in range(0, width, TILE):
        at = slice(start, start + TILE)
        joined[:, at] = (
            kept[:, at]
            + got[:, at].astype(jnp.float32)
            + jnp.dot(coefficient[0], up_here[:, at], preferred_element_type=jnp.float32)
            + jnp.dot(coefficient[1], up_there[:, at], preferred_element_type=jnp.float32)
        )
    here = pl.ds(pl.multiple_of(high * block, block), block)
    there = pl.ds(pl.multiple_of((1 - high) * block, block), block)
    sent[...] = joined[there, :].astype(sent.dtype)
    total[...] = joined[here, :] + residual[...].astype(jnp.float32)


def join_phase(ids, near, far, up_here, up_there, kept, got, residual):
    return pl.pallas_call(
        join_kernel,
        out_shape=(
            jax.ShapeDtypeStruct(residual.shape, jnp.bfloat16),
            jax.ShapeDtypeStruct(residual.shape, jnp.float32),
        ),
        in_specs=[VMEM] * 8,
        out_specs=(VMEM,) * 2,
        scratch_shapes=[pltpu.VMEM(kept.shape, kept.dtype)],
        compiler_params=pltpu.CompilerParams(vmem_limit_bytes=8 << 20),
        name="join",
    )(ids, near, far, up_here, up_there, kept, got, residual)


def finish_kernel(total, got, mixed):
    mixed[...] = (total[...] + got[...].astype(jnp.float32)).astype(mixed.dtype)


def finish_phase(total, got):
    return pl.pallas_call(
        finish_kernel,
        out_shape=jax.ShapeDtypeStruct(total.shape, got.dtype),
        in_specs=[VMEM] * 2,
        out_specs=VMEM,
        compiler_params=pltpu.CompilerParams(vmem_limit_bytes=8 << 20),
        name="finish",
    )(total, got)


def swap(value, axis, bit=1):
    return lax.ppermute(value, axis, [(i, i ^ bit) for i in range(lax.axis_size(axis))])


def to_holders(value, flip):
    pairs = []
    for tp in range(4):
        for page in range(2):
            for sub in range(2):
                to = (2 * page + (tp % 2 ^ flip), tp // 2 ^ sub, sub)
                pairs.append((4 * tp + 2 * page + sub, 4 * to[0] + 2 * to[1] + to[2]))
    return lax.ppermute(value, ("tp",) + PS, pairs)


def four_by_four(hidden, adapter_ids, weight, rank_down, rank_up, residual):
    ids = adapter_ids[None]
    up = rank_up[0]
    up_there = swap(up, "tp", 1)
    packed, sent, kept = stream_phase(hidden, jnp.swapaxes(rank_down, 1, 2)[0], weight)
    sent, up_there = lax.optimization_barrier((sent, up_there))
    got = swap(sent, "tp", 1)
    same, flipped = merge_phase(ids, packed, swap(packed, "sub"))
    low = to_holders(same, 0) + to_holders(flipped, 1)
    sent, total = join_phase(ids, low, swap(low, "sub"), up, up_there, kept, got, residual)
    return finish_phase(total, swap(sent, "tp", 2))


def any_size(hidden_units, adapter_ids, down_projection_weight, rank_down, rank_up, residual):
    owned_count = rank_down.shape[0]
    first_owned = lax.axis_index(PS) * owned_count
    chosen = (
        (adapter_ids - first_owned)[:, None] == jnp.arange(owned_count, dtype=jnp.int32)[None, :]
    ).astype(jnp.float32)
    projected = jnp.einsum(
        "rf,afk->rak", hidden_units, rank_down, preferred_element_type=jnp.float32
    )
    partial_low = jnp.einsum("rak,ra->rk", projected, chosen)
    low_rank = lax.psum(partial_low, ("tp",) + PS).astype(jnp.bfloat16)
    held_count, rank_width, columns = rank_up.shape
    first_held = lax.axis_index("tp") * held_count
    picked = (
        (adapter_ids - first_held)[:, None] == jnp.arange(held_count, dtype=jnp.int32)[None, :]
    ).astype(jnp.bfloat16)
    coefficient = (picked[:, :, None] * low_rank[:, None, :]).reshape(
        -1, held_count * rank_width
    )
    term = jnp.dot(
        hidden_units, down_projection_weight, preferred_element_type=jnp.float32
    ) + jnp.dot(
        coefficient,
        rank_up.reshape(held_count * rank_width, columns),
        preferred_element_type=jnp.float32,
    )
    summed = lax.psum_scatter(
        term.astype(jnp.bfloat16), "tp", scatter_dimension=0, tiled=True
    ).astype(jnp.float32)
    return (residual.astype(jnp.float32) + summed).astype(jnp.bfloat16)


def on_device(hidden_units, adapter_ids, down_projection_weight, rank_down, rank_up, residual):
    sizes = [lax.axis_size(axis) for axis in ("tp",) + PS]
    fits = (
        sizes[0] == 4
        and sizes[1] == 2
        and sizes[2] == 2
        and rank_down.shape[0] == 1
        and rank_up.shape[0] == 1
        and residual.shape == (16, 6 * TILE)
        and hidden_units.shape[1] % (GROUP * PART) == 0
        and hidden_units.shape[1] >= SLOTS * GROUP * PART
    )
    form = four_by_four if fits else any_size
    return form(hidden_units, adapter_ids, down_projection_weight, rank_down, rank_up, residual)


def solution(mesh):
    placed = (
        P("parts", "tp"),
        P("parts"),
        P("tp", ("page", "sub")),
        P(("parts", "page", "sub"), "tp", None),
        P(("parts", "tp"), None, ("page", "sub")),
        P(("parts", "tp"), ("page", "sub")),
    )
    return jax.shard_map(
        on_device,
        mesh=mesh,
        in_specs=placed,
        out_specs=P(("parts", "tp"), ("page", "sub")),
        check_vma=False,
    )
```

```python
import functools

import jax
import jax.numpy as jnp
from jax import lax
from jax.experimental import pallas as pl
from jax.experimental.pallas import tpu as pltpu
from jax.sharding import PartitionSpec as P

PART = 256
GROUP = 3
SLOTS = 5
HELD = 3
TILE = 512
PS = ("page", "sub")
VMEM = pl.BlockSpec(memory_space=pltpu.VMEM)
HBM = pl.BlockSpec(memory_space=pltpu.HBM)


def column_of(ids_row):
    rows = ids_row.shape[1]
    down = lax.broadcasted_iota(jnp.int32, (rows, rows), 0)
    across = lax.broadcasted_iota(jnp.int32, (rows, rows), 1)
    spread = jnp.broadcast_to(ids_row, (rows, rows))
    return jnp.sum(
        jnp.where(down == across, spread.astype(jnp.float32), 0.0), axis=1, keepdims=True
    )


def low_kernel(hidden, rank_down, packed, hidden_here, down_here, got):
    copies = [
        pltpu.make_async_copy(hidden, hidden_here, got.at[0]),
        pltpu.make_async_copy(rank_down, down_here, got.at[1]),
    ]
    for copy in copies:
        copy.start()
    for copy in copies:
        copy.wait()
    low = lax.dot_general(
        hidden_here[...],
        down_here[...],
        (((1,), (1,)), ((), ())),
        preferred_element_type=jnp.float32,
    )
    half = low.shape[0] // 2
    packed[...] = jnp.concatenate([low[:half], low[half:]], axis=1)


def low_phase(hidden, rank_down):
    rows, depth = hidden.shape
    rank = rank_down.shape[0]
    return pl.pallas_call(
        low_kernel,
        out_shape=(
            jax.ShapeDtypeStruct((rows // 2, 2 * rank), jnp.float32),
            jax.ShapeDtypeStruct(hidden.shape, hidden.dtype),
        ),
        in_specs=[HBM] * 2,
        out_specs=(VMEM,) * 2,
        scratch_shapes=[
            pltpu.VMEM(rank_down.shape, rank_down.dtype),
            pltpu.SemaphoreType.DMA((2,)),
        ],
        compiler_params=pltpu.CompilerParams(vmem_limit_bytes=52 << 20),
        cost_estimate=pl.CostEstimate(
            flops=2 * rows * depth * rank,
            bytes_accessed=2 * depth * (rank + rows),
            transcendentals=0,
        ),
        name="low_rank",
    )(hidden, rank_down)


def stream_kernel(hidden, slab, weight, sent, kept, total, held, arrived):
    groups = weight.shape[0] // (PART * GROUP)
    width = weight.shape[1]
    deep = PART * GROUP

    def part_copy(group, part):
        rows = pl.ds(pl.multiple_of(group * deep + part * PART, PART), PART)
        slot = lax.rem(group, SLOTS)
        there = pl.ds(pl.multiple_of(slot * deep + part * PART, PART), PART)
        return pltpu.make_async_copy(
            weight.at[rows], held.at[there], arrived.at[slot * GROUP + part]
        )

    @pl.loop(HELD, HELD + SLOTS - 1)
    def _(group):
        for part in range(GROUP):
            part_copy(group, part).start()

    total[...] = jnp.zeros_like(total)

    def add(rows, at, depth):
        for start in range(0, width, TILE):
            columns = slice(start, start + TILE)
            total[:, columns] += jnp.dot(
                hidden[:, pl.ds(at, depth)],
                rows[:, columns],
                preferred_element_type=jnp.float32,
            )

    @pl.loop(0, HELD)
    def _(group):
        at = pl.multiple_of(group * deep, deep)
        add(slab.at[pl.ds(at, deep)], at, deep)

    def add_part(group, part, depth):
        at = pl.multiple_of(group * deep + part * PART, PART)
        slot = pl.multiple_of(lax.rem(group, SLOTS) * deep + part * PART, PART)
        add(held.at[pl.ds(slot, depth)], at, depth)

    @pl.loop(HELD, groups - 1)
    def _(group):
        @pl.when(group + SLOTS - 1 < groups)
        def _():
            for part in range(GROUP):
                part_copy(group + SLOTS - 1, part).start()

        for part in range(GROUP):
            part_copy(group, part).wait()
        add_part(group, 0, deep)

    for part in range(GROUP):
        part_copy(groups - 1, part).wait()
        add_part(groups - 1, part, PART)
    split_rows(total, slice(0, width), sent, kept)


def stream_phase(hidden, weight):
    rows, depth = hidden.shape
    width = weight.shape[1]
    return pl.pallas_call(
        stream_kernel,
        out_shape=(
            jax.ShapeDtypeStruct((rows // 2, width), jnp.bfloat16),
            jax.ShapeDtypeStruct((rows // 2, width), jnp.float32),
        ),
        in_specs=[VMEM, VMEM, HBM],
        out_specs=(VMEM,) * 2,
        scratch_shapes=[
            pltpu.VMEM((rows, width), jnp.float32),
            pltpu.VMEM((SLOTS * GROUP * PART, width), weight.dtype),
            pltpu.SemaphoreType.DMA((SLOTS * GROUP,)),
        ],
        compiler_params=pltpu.CompilerParams(vmem_limit_bytes=28 << 20),
        cost_estimate=pl.CostEstimate(
            flops=2 * rows * depth * width, bytes_accessed=2 * depth * width, transcendentals=0
        ),
        name="base",
    )(hidden, weight[: HELD * GROUP * PART], weight)


def split_rows(total, at, sent, kept):
    block = total.shape[0] // 4
    bit = lax.rem(lax.axis_index("tp"), 2)
    for half in range(2):
        rows = pl.ds(half * block, block)
        there = pl.ds(pl.multiple_of((2 * half + 1 - bit) * block, block), block)
        here = pl.ds(pl.multiple_of((2 * half + bit) * block, block), block)
        sent[rows, at] = total[there, :].astype(sent.dtype)
        kept[rows, at] = total[here, :]


def unpacked(packed):
    rank = packed.shape[1] // 2
    return jnp.concatenate([packed[:, :rank], packed[:, rank:]], axis=0)


def merge_kernel(ids, own, other, same, flipped):
    page, sub = lax.axis_index("page"), lax.axis_index("sub")
    adapter = column_of(ids[...])
    mine = (2 * page + sub).astype(jnp.float32)
    theirs = (2 * page + 1 - sub).astype(jnp.float32)
    low = jnp.where(
        adapter == mine,
        unpacked(own[...]),
        jnp.where(adapter == theirs, unpacked(other[...]), 0.0),
    )
    block = low.shape[0] // 4
    rows = [low[index * block : (index + 1) * block] for index in range(4)]
    even = jnp.concatenate([rows[0], rows[2]], axis=1)
    odd = jnp.concatenate([rows[1], rows[3]], axis=1)
    bit = lax.rem(lax.axis_index("tp"), 2)
    same[...] = jnp.where(bit == 0, even, odd)
    flipped[...] = jnp.where(bit == 0, odd, even)


def merge_phase(ids, own, other):
    shape = jax.ShapeDtypeStruct((own.shape[0] // 2, own.shape[1]), own.dtype)
    return pl.pallas_call(
        merge_kernel,
        out_shape=(shape, shape),
        in_specs=[VMEM] * 3,
        out_specs=(VMEM,) * 2,
        compiler_params=pltpu.CompilerParams(vmem_limit_bytes=4 << 20),
        name="merge_low_rank",
    )(ids, own, other)


def join_kernel(ids, near, far, up_here, up_there, kept, got, residual, sent, total, joined):
    block = residual.shape[0]
    tp = lax.axis_index("tp")
    high, bit = lax.div(tp, 2), lax.rem(tp, 2)
    every = column_of(ids[...])
    parts = [every[index * block : (index + 1) * block] for index in range(4)]
    adapter = jnp.concatenate(
        [jnp.where(bit == 0, parts[half], parts[half + 1]) for half in (0, 2)], axis=0
    )
    low = unpacked(near[...] + far[...])
    coefficient = [
        jnp.where(adapter == index.astype(jnp.float32), low, 0.0).astype(jnp.bfloat16)
        for index in (tp, tp + 1 - 2 * bit)
    ]
    width = residual.shape[1]
    for start in range(0, width, TILE):
        at = slice(start, start + TILE)
        joined[:, at] = (
            kept[:, at]
            + got[:, at].astype(jnp.float32)
            + jnp.dot(coefficient[0], up_here[:, at], preferred_element_type=jnp.float32)
            + jnp.dot(coefficient[1], up_there[:, at], preferred_element_type=jnp.float32)
        )
    here = pl.ds(pl.multiple_of(high * block, block), block)
    there = pl.ds(pl.multiple_of((1 - high) * block, block), block)
    sent[...] = joined[there, :].astype(sent.dtype)
    total[...] = joined[here, :] + residual[...].astype(jnp.float32)


def join_phase(ids, near, far, up_here, up_there, kept, got, residual):
    return pl.pallas_call(
        join_kernel,
        out_shape=(
            jax.ShapeDtypeStruct(residual.shape, jnp.bfloat16),
            jax.ShapeDtypeStruct(residual.shape, jnp.float32),
        ),
        in_specs=[VMEM] * 8,
        out_specs=(VMEM,) * 2,
        scratch_shapes=[pltpu.VMEM(kept.shape, kept.dtype)],
        compiler_params=pltpu.CompilerParams(vmem_limit_bytes=8 << 20),
        name="join",
    )(ids, near, far, up_here, up_there, kept, got, residual)


def finish_kernel(total, got, mixed):
    mixed[...] = (total[...] + got[...].astype(jnp.float32)).astype(mixed.dtype)


def finish_phase(total, got):
    return pl.pallas_call(
        finish_kernel,
        out_shape=jax.ShapeDtypeStruct(total.shape, got.dtype),
        in_specs=[VMEM] * 2,
        out_specs=VMEM,
        compiler_params=pltpu.CompilerParams(vmem_limit_bytes=8 << 20),
        name="finish",
    )(total, got)


def swap(value, axis, bit=1):
    return lax.ppermute(value, axis, [(i, i ^ bit) for i in range(lax.axis_size(axis))])


def to_holders(value, flip):
    pairs = []
    for tp in range(4):
        for page in range(2):
            for sub in range(2):
                to = (2 * page + (tp % 2 ^ flip), tp // 2 ^ sub, sub)
                pairs.append((4 * tp + 2 * page + sub, 4 * to[0] + 2 * to[1] + to[2]))
    return lax.ppermute(value, ("tp",) + PS, pairs)


def four_by_four(hidden, adapter_ids, weight, rank_down, rank_up, residual):
    ids = adapter_ids[None]
    up = rank_up[0]
    packed, hidden = low_phase(hidden, jnp.swapaxes(rank_down, 1, 2)[0])
    up_there = swap(up, "tp", 1)
    same, flipped = merge_phase(ids, packed, swap(packed, "sub"))
    low, flipped = to_holders(same, 0), to_holders(flipped, 1)
    sent, kept = stream_phase(hidden, weight)
    sent, up_there, low, flipped = lax.optimization_barrier((sent, up_there, low, flipped))
    got = swap(sent, "tp", 1)
    low = low + flipped
    sent, total = join_phase(ids, low, swap(low, "sub"), up, up_there, kept, got, residual)
    return finish_phase(total, swap(sent, "tp", 2))


def any_size(hidden_units, adapter_ids, down_projection_weight, rank_down, rank_up, residual):
    owned_count = rank_down.shape[0]
    first_owned = lax.axis_index(PS) * owned_count
    chosen = (
        (adapter_ids - first_owned)[:, None] == jnp.arange(owned_count, dtype=jnp.int32)[None, :]
    ).astype(jnp.float32)
    projected = jnp.einsum(
        "rf,afk->rak", hidden_units, rank_down, preferred_element_type=jnp.float32
    )
    partial_low = jnp.einsum("rak,ra->rk", projected, chosen)
    low_rank = lax.psum(partial_low, ("tp",) + PS).astype(jnp.bfloat16)
    held_count, rank_width, columns = rank_up.shape
    first_held = lax.axis_index("tp") * held_count
    picked = (
        (adapter_ids - first_held)[:, None] == jnp.arange(held_count, dtype=jnp.int32)[None, :]
    ).astype(jnp.bfloat16)
    coefficient = (picked[:, :, None] * low_rank[:, None, :]).reshape(
        -1, held_count * rank_width
    )
    term = jnp.dot(
        hidden_units, down_projection_weight, preferred_element_type=jnp.float32
    ) + jnp.dot(
        coefficient,
        rank_up.reshape(held_count * rank_width, columns),
        preferred_element_type=jnp.float32,
    )
    summed = lax.psum_scatter(
        term.astype(jnp.bfloat16), "tp", scatter_dimension=0, tiled=True
    ).astype(jnp.float32)
    return (residual.astype(jnp.float32) + summed).astype(jnp.bfloat16)


def on_device(hidden_units, adapter_ids, down_projection_weight, rank_down, rank_up, residual):
    sizes = [lax.axis_size(axis) for axis in ("tp",) + PS]
    fits = (
        sizes[0] == 4
        and sizes[1] == 2
        and sizes[2] == 2
        and rank_down.shape[0] == 1
        and rank_up.shape[0] == 1
        and residual.shape == (16, 6 * TILE)
        and hidden_units.shape[1] % (GROUP * PART) == 0
        and hidden_units.shape[1] >= SLOTS * GROUP * PART
    )
    form = four_by_four if fits else any_size
    return form(hidden_units, adapter_ids, down_projection_weight, rank_down, rank_up, residual)


def solution(mesh):
    placed = (
        P("parts", "tp"),
        P("parts"),
        P("tp", ("page", "sub")),
        P(("parts", "page", "sub"), "tp", None),
        P(("parts", "tp"), None, ("page", "sub")),
        P(("parts", "tp"), ("page", "sub")),
    )
    return jax.shard_map(
        on_device,
        mesh=mesh,
        in_specs=placed,
        out_specs=P(("parts", "tp"), ("page", "sub")),
        check_vma=False,
    )
```

```python
import functools

import jax
import jax.numpy as jnp
from jax import lax
from jax.experimental import pallas as pl
from jax.experimental.pallas import tpu as pltpu
from jax.sharding import PartitionSpec as P

WIDTHS = (2304, 768)
DEPTH = 768
PS = ("page", "sub")
VMEM = pl.BlockSpec(memory_space=pltpu.VMEM)
HBM = pl.BlockSpec(memory_space=pltpu.HBM)


def column_of(ids_row):
    rows = ids_row.shape[1]
    down = lax.broadcasted_iota(jnp.int32, (rows, rows), 0)
    across = lax.broadcasted_iota(jnp.int32, (rows, rows), 1)
    spread = jnp.broadcast_to(ids_row, (rows, rows))
    return jnp.sum(
        jnp.where(down == across, spread.astype(jnp.float32), 0.0), axis=1, keepdims=True
    )


def deep(k):
    return pl.ds(pl.multiple_of(k * DEPTH, DEPTH), DEPTH)


def weight_copies(weight, held, arrived, start, width):
    def copy(k):
        return pltpu.make_async_copy(
            weight.at[deep(k), pl.ds(start, width)], held.at[deep(k)], arrived.at[k]
        )

    return copy


def low_kernel(hidden, rank_down, low, hidden_here, down_here, got):
    copies = [
        pltpu.make_async_copy(hidden, hidden_here, got.at[0]),
        pltpu.make_async_copy(rank_down, down_here, got.at[1]),
    ]
    for copy in copies:
        copy.start()
    for copy in copies:
        copy.wait()
    low[...] = lax.dot_general(
        hidden_here[...],
        down_here[...],
        (((1,), (1,)), ((), ())),
        preferred_element_type=jnp.float32,
    )


def low_phase(hidden, rank_down):
    rows, depth = hidden.shape
    rank = rank_down.shape[0]
    return pl.pallas_call(
        low_kernel,
        out_shape=(
            jax.ShapeDtypeStruct((rows, rank), jnp.float32),
            jax.ShapeDtypeStruct(hidden.shape, hidden.dtype),
        ),
        in_specs=[HBM] * 2,
        out_specs=(VMEM,) * 2,
        scratch_shapes=[
            pltpu.VMEM(rank_down.shape, rank_down.dtype),
            pltpu.SemaphoreType.DMA((2,)),
        ],
        compiler_params=pltpu.CompilerParams(vmem_limit_bytes=52 << 20),
        cost_estimate=pl.CostEstimate(
            flops=2 * rows * depth * rank,
            bytes_accessed=2 * depth * (rank + rows),
            transcendentals=0,
        ),
        name="low_rank",
    )(hidden, rank_down)


def stream_dot(hidden, weight, total, held, arrived, start):
    steps = weight.shape[0] // DEPTH
    copy = weight_copies(weight, held, arrived, start, total.shape[1])

    @pl.loop(0, steps)
    def _(k):
        copy(k).start()

    total[...] = jnp.zeros_like(total)

    @pl.loop(0, steps)
    def _(k):
        copy(k).wait()
        total[...] += jnp.dot(hidden[:, deep(k)], held[deep(k)], preferred_element_type=jnp.float32)


def base_kernel(start, hidden, weight, base, held, arrived):
    stream_dot(hidden, weight, base, held, arrived, start)


def base_phase(hidden, weight, start, width):
    rows, depth = hidden.shape
    return pl.pallas_call(
        functools.partial(base_kernel, start),
        out_shape=jax.ShapeDtypeStruct((rows, width), jnp.float32),
        in_specs=[VMEM, HBM],
        out_specs=VMEM,
        scratch_shapes=[
            pltpu.VMEM((depth, width), weight.dtype),
            pltpu.SemaphoreType.DMA((depth // DEPTH,)),
        ],
        compiler_params=pltpu.CompilerParams(vmem_limit_bytes=42 << 20),
        cost_estimate=pl.CostEstimate(
            flops=2 * rows * depth * width, bytes_accessed=2 * depth * width, transcendentals=0
        ),
        name="base",
    )(hidden, weight)


def split_rows(total, at, sent, kept):
    block = total.shape[0] // 4
    bit = lax.rem(lax.axis_index("tp"), 2)
    for half in range(2):
        rows = pl.ds(half * block, block)
        there = pl.ds(pl.multiple_of((2 * half + 1 - bit) * block, block), block)
        here = pl.ds(pl.multiple_of((2 * half + bit) * block, block), block)
        sent[rows, at] = total[there, :].astype(sent.dtype)
        kept[rows, at] = total[here, :]


def adapter_term(low, up):
    return jnp.dot(low.astype(jnp.bfloat16), up, preferred_element_type=jnp.float32)


def correct_kernel(ids, low_a, low_b, low_c, low_d, up, base, low, sent, kept, total):
    held = column_of(ids[...]) == lax.axis_index("tp").astype(jnp.float32)
    low[...] = jnp.where(held, (low_a[...] + low_b[...]) + (low_c[...] + low_d[...]), 0.0)
    width = base.shape[1]
    total[...] = base[...] + adapter_term(low[...], up[:, :width])
    split_rows(total, slice(0, width), sent, kept)


def correct_phase(ids, lows, up, base):
    rows, rank = lows[0].shape
    width = base.shape[1]
    return pl.pallas_call(
        correct_kernel,
        out_shape=(
            jax.ShapeDtypeStruct((rows, rank), jnp.float32),
            jax.ShapeDtypeStruct((rows // 2, width), jnp.bfloat16),
            jax.ShapeDtypeStruct((rows // 2, width), jnp.float32),
        ),
        in_specs=[VMEM] * 7,
        out_specs=(VMEM,) * 3,
        scratch_shapes=[pltpu.VMEM((rows, width), jnp.float32)],
        compiler_params=pltpu.CompilerParams(vmem_limit_bytes=8 << 20),
        name="adapter_term",
    )(ids, *lows, up, base)


def last_kernel(start, hidden, weight, low, up, sent, kept, total, held, arrived):
    stream_dot(hidden, weight, total, held, arrived, start)
    width = total.shape[1]
    total[...] += adapter_term(low[...], up[:, start : start + width])
    split_rows(total, slice(0, width), sent, kept)


def last_phase(hidden, weight, low, up, start, width):
    rows, depth = hidden.shape
    return pl.pallas_call(
        functools.partial(last_kernel, start),
        out_shape=(
            jax.ShapeDtypeStruct((rows // 2, width), jnp.bfloat16),
            jax.ShapeDtypeStruct((rows // 2, width), jnp.float32),
        ),
        in_specs=[VMEM, HBM, VMEM, VMEM],
        out_specs=(VMEM, VMEM),
        scratch_shapes=[
            pltpu.VMEM((rows, width), jnp.float32),
            pltpu.VMEM((depth, width), weight.dtype),
            pltpu.SemaphoreType.DMA((depth // DEPTH,)),
        ],
        compiler_params=pltpu.CompilerParams(vmem_limit_bytes=32 << 20),
        cost_estimate=pl.CostEstimate(
            flops=2 * rows * depth * width, bytes_accessed=2 * depth * width, transcendentals=0
        ),
        name="last_base",
    )(hidden, weight, low, up)


def pair_kernel(kept, got, sent, total):
    block = kept.shape[0] // 2
    high = lax.div(lax.axis_index("tp"), 2)
    here = pl.ds(pl.multiple_of(high * block, block), block)
    there = pl.ds(pl.multiple_of((1 - high) * block, block), block)
    sent[...] = (kept[there, :] + got[there, :].astype(jnp.float32)).astype(sent.dtype)
    total[...] = kept[here, :] + got[here, :].astype(jnp.float32)


def pair_phase(kept, got):
    rows, width = kept.shape
    return pl.pallas_call(
        pair_kernel,
        out_shape=(
            jax.ShapeDtypeStruct((rows // 2, width), jnp.bfloat16),
            jax.ShapeDtypeStruct((rows // 2, width), jnp.float32),
        ),
        in_specs=[VMEM] * 2,
        out_specs=(VMEM,) * 2,
        compiler_params=pltpu.CompilerParams(vmem_limit_bytes=8 << 20),
        name="pair_sum",
    )(kept, got)


def finish_kernel(residual, total_one, got_one, total_two, got_two, mixed):
    start = 0
    for total, got in ((total_one, got_one), (total_two, got_two)):
        at = slice(start, start + total.shape[1])
        mixed[:, at] = (
            residual[:, at].astype(jnp.float32) + total[...] + got[...].astype(jnp.float32)
        ).astype(mixed.dtype)
        start = at.stop


def finish_phase(residual, *terms):
    return pl.pallas_call(
        finish_kernel,
        out_shape=jax.ShapeDtypeStruct(residual.shape, residual.dtype),
        in_specs=[VMEM] * 5,
        out_specs=VMEM,
        compiler_params=pltpu.CompilerParams(vmem_limit_bytes=8 << 20),
        name="finish",
    )(residual, *terms)


def swap(value, bit):
    return lax.ppermute(value, "tp", [(i, i ^ bit) for i in range(lax.axis_size("tp"))])


def four_by_four(hidden, adapter_ids, weight, rank_down, rank_up, residual):
    up = rank_up[0]
    one, two = WIDTHS
    low, hidden = low_phase(hidden, jnp.swapaxes(rank_down, 1, 2)[0])
    lows = []
    for j in range(4):
        pairs = [(t * 4 + a, a * 4 + (t + j) % 4) for t in range(4) for a in range(4)]
        lows.append(lax.ppermute(low, ("tp",) + PS, pairs))
    base = base_phase(hidden, weight, 0, one)
    low, sent, kept = correct_phase(adapter_ids[None], lows, up, base)
    got = swap(sent, 1)
    sent_last, kept_last = last_phase(hidden, weight, low, up, one, two)
    got_last = swap(sent_last, 1)
    sent, total = pair_phase(kept, got)
    got = swap(sent, 2)
    sent_last, total_last = pair_phase(kept_last, got_last)
    got_last = swap(sent_last, 2)
    return finish_phase(residual, total, got, total_last, got_last)


def any_size(hidden_units, adapter_ids, down_projection_weight, rank_down, rank_up, residual):
    owned_count = rank_down.shape[0]
    first_owned = lax.axis_index(PS) * owned_count
    chosen = (
        (adapter_ids - first_owned)[:, None] == jnp.arange(owned_count, dtype=jnp.int32)[None, :]
    ).astype(jnp.float32)
    projected = jnp.einsum(
        "rf,afk->rak", hidden_units, rank_down, preferred_element_type=jnp.float32
    )
    partial_low = jnp.einsum("rak,ra->rk", projected, chosen)
    low_rank = lax.psum(partial_low, ("tp",) + PS).astype(jnp.bfloat16)
    held_count, rank_width, columns = rank_up.shape
    first_held = lax.axis_index("tp") * held_count
    picked = (
        (adapter_ids - first_held)[:, None] == jnp.arange(held_count, dtype=jnp.int32)[None, :]
    ).astype(jnp.bfloat16)
    coefficient = (picked[:, :, None] * low_rank[:, None, :]).reshape(
        -1, held_count * rank_width
    )
    term = jnp.dot(
        hidden_units, down_projection_weight, preferred_element_type=jnp.float32
    ) + jnp.dot(
        coefficient,
        rank_up.reshape(held_count * rank_width, columns),
        preferred_element_type=jnp.float32,
    )
    summed = lax.psum_scatter(
        term.astype(jnp.bfloat16), "tp", scatter_dimension=0, tiled=True
    ).astype(jnp.float32)
    return (residual.astype(jnp.float32) + summed).astype(jnp.bfloat16)


def on_device(hidden_units, adapter_ids, down_projection_weight, rank_down, rank_up, residual):
    sizes = [lax.axis_size(axis) for axis in ("tp",) + PS]
    fits = (
        sizes[0] == 4
        and sizes[1] * sizes[2] == 4
        and rank_down.shape[0] == 1
        and rank_up.shape[0] == 1
        and residual.shape == (16, sum(WIDTHS))
        and hidden_units.shape[1] % DEPTH == 0
    )
    form = four_by_four if fits else any_size
    return form(hidden_units, adapter_ids, down_projection_weight, rank_down, rank_up, residual)


def solution(mesh):
    placed = (
        P("parts", "tp"),
        P("parts"),
        P("tp", ("page", "sub")),
        P(("parts", "page", "sub"), "tp", None),
        P(("parts", "tp"), None, ("page", "sub")),
        P(("parts", "tp"), ("page", "sub")),
    )
    return jax.shard_map(
        on_device,
        mesh=mesh,
        in_specs=placed,
        out_specs=P(("parts", "tp"), ("page", "sub")),
        check_vma=False,
    )
```

```python
import functools

import jax
import jax.numpy as jnp
from jax import lax
from jax.experimental import pallas as pl
from jax.experimental.pallas import tpu as pltpu
from jax.sharding import PartitionSpec as P

WIDTHS = (2304, 768)
DEPTH = 768
PS = ("page", "sub")
VMEM = pl.BlockSpec(memory_space=pltpu.VMEM)
HBM = pl.BlockSpec(memory_space=pltpu.HBM)


def column_of(ids_row):
    rows = ids_row.shape[1]
    down = lax.broadcasted_iota(jnp.int32, (rows, rows), 0)
    across = lax.broadcasted_iota(jnp.int32, (rows, rows), 1)
    spread = jnp.broadcast_to(ids_row, (rows, rows))
    return jnp.sum(
        jnp.where(down == across, spread.astype(jnp.float32), 0.0), axis=1, keepdims=True
    )


def deep(k):
    return pl.ds(pl.multiple_of(k * DEPTH, DEPTH), DEPTH)


def weight_copies(weight, held, arrived, start, width):
    def copy(k):
        return pltpu.make_async_copy(
            weight.at[deep(k), pl.ds(start, width)], held.at[deep(k)], arrived.at[k]
        )

    return copy


def low_kernel(hidden, rank_down, packed, hidden_here, down_here, got):
    copies = [
        pltpu.make_async_copy(hidden, hidden_here, got.at[0]),
        pltpu.make_async_copy(rank_down, down_here, got.at[1]),
    ]
    for copy in copies:
        copy.start()
    for copy in copies:
        copy.wait()
    low = lax.dot_general(
        hidden_here[...],
        down_here[...],
        (((1,), (1,)), ((), ())),
        preferred_element_type=jnp.float32,
    )
    half = low.shape[0] // 2
    block = jnp.concatenate([low[:half], low[half:]], axis=1)
    for to in range(packed.shape[0]):
        packed[to] = block


def low_phase(hidden, rank_down):
    rows, depth = hidden.shape
    rank = rank_down.shape[0]
    return pl.pallas_call(
        low_kernel,
        out_shape=(
            jax.ShapeDtypeStruct((16, rows // 2, 2 * rank), jnp.float32),
            jax.ShapeDtypeStruct(hidden.shape, hidden.dtype),
        ),
        in_specs=[HBM] * 2,
        out_specs=(VMEM,) * 2,
        scratch_shapes=[
            pltpu.VMEM(rank_down.shape, rank_down.dtype),
            pltpu.SemaphoreType.DMA((2,)),
        ],
        compiler_params=pltpu.CompilerParams(vmem_limit_bytes=52 << 20),
        cost_estimate=pl.CostEstimate(
            flops=2 * rows * depth * rank,
            bytes_accessed=2 * depth * (rank + rows),
            transcendentals=0,
        ),
        name="low_rank",
    )(hidden, rank_down)


def stream_dot(hidden, weight, total, held, arrived, start):
    steps = weight.shape[0] // DEPTH
    copy = weight_copies(weight, held, arrived, start, total.shape[1])

    @pl.loop(0, steps)
    def _(k):
        copy(k).start()

    total[...] = jnp.zeros_like(total)

    @pl.loop(0, steps)
    def _(k):
        copy(k).wait()
        total[...] += jnp.dot(hidden[:, deep(k)], held[deep(k)], preferred_element_type=jnp.float32)


def base_kernel(start, hidden, weight, base, held, arrived):
    stream_dot(hidden, weight, base, held, arrived, start)


def base_phase(hidden, weight, start, width):
    rows, depth = hidden.shape
    return pl.pallas_call(
        functools.partial(base_kernel, start),
        out_shape=jax.ShapeDtypeStruct((rows, width), jnp.float32),
        in_specs=[VMEM, HBM],
        out_specs=VMEM,
        scratch_shapes=[
            pltpu.VMEM((depth, width), weight.dtype),
            pltpu.SemaphoreType.DMA((depth // DEPTH,)),
        ],
        compiler_params=pltpu.CompilerParams(vmem_limit_bytes=42 << 20),
        cost_estimate=pl.CostEstimate(
            flops=2 * rows * depth * width, bytes_accessed=2 * depth * width, transcendentals=0
        ),
        name="base",
    )(hidden, weight)


def split_rows(total, at, sent, kept):
    block = total.shape[0] // 4
    bit = lax.rem(lax.axis_index("tp"), 2)
    for half in range(2):
        rows = pl.ds(half * block, block)
        there = pl.ds(pl.multiple_of((2 * half + 1 - bit) * block, block), block)
        here = pl.ds(pl.multiple_of((2 * half + bit) * block, block), block)
        sent[rows, at] = total[there, :].astype(sent.dtype)
        kept[rows, at] = total[here, :]


def adapter_term(low, up):
    return jnp.dot(low.astype(jnp.bfloat16), up, preferred_element_type=jnp.float32)


def correct_kernel(ids, packed, up, base, low, sent, kept, total):
    tp = lax.axis_index("tp")
    summed = packed[tp]
    for source in range(1, 4):
        summed = summed + packed[4 * source + tp]
    rank = low.shape[1]
    summed = jnp.concatenate([summed[:, :rank], summed[:, rank:]], axis=0)
    held = column_of(ids[...]) == tp.astype(jnp.float32)
    low[...] = jnp.where(held, summed, 0.0)
    width = base.shape[1]
    total[...] = base[...] + adapter_term(low[...], up[:, :width])
    split_rows(total, slice(0, width), sent, kept)


def correct_phase(ids, packed, up, base):
    rows = base.shape[0]
    rank = up.shape[0]
    width = base.shape[1]
    return pl.pallas_call(
        correct_kernel,
        out_shape=(
            jax.ShapeDtypeStruct((rows, rank), jnp.float32),
            jax.ShapeDtypeStruct((rows // 2, width), jnp.bfloat16),
            jax.ShapeDtypeStruct((rows // 2, width), jnp.float32),
        ),
        in_specs=[VMEM] * 4,
        out_specs=(VMEM,) * 3,
        scratch_shapes=[pltpu.VMEM((rows, width), jnp.float32)],
        compiler_params=pltpu.CompilerParams(vmem_limit_bytes=8 << 20),
        name="adapter_term",
    )(ids, packed, up, base)


def last_kernel(start, hidden, weight, low, up, sent, kept, total, held, arrived):
    stream_dot(hidden, weight, total, held, arrived, start)
    width = total.shape[1]
    total[...] += adapter_term(low[...], up[:, start : start + width])
    split_rows(total, slice(0, width), sent, kept)


def last_phase(hidden, weight, low, up, start, width):
    rows, depth = hidden.shape
    return pl.pallas_call(
        functools.partial(last_kernel, start),
        out_shape=(
            jax.ShapeDtypeStruct((rows // 2, width), jnp.bfloat16),
            jax.ShapeDtypeStruct((rows // 2, width), jnp.float32),
        ),
        in_specs=[VMEM, HBM, VMEM, VMEM],
        out_specs=(VMEM, VMEM),
        scratch_shapes=[
            pltpu.VMEM((rows, width), jnp.float32),
            pltpu.VMEM((depth, width), weight.dtype),
            pltpu.SemaphoreType.DMA((depth // DEPTH,)),
        ],
        compiler_params=pltpu.CompilerParams(vmem_limit_bytes=32 << 20),
        cost_estimate=pl.CostEstimate(
            flops=2 * rows * depth * width, bytes_accessed=2 * depth * width, transcendentals=0
        ),
        name="last_base",
    )(hidden, weight, low, up)


def pair_kernel(kept, got, sent, total):
    block = kept.shape[0] // 2
    high = lax.div(lax.axis_index("tp"), 2)
    here = pl.ds(pl.multiple_of(high * block, block), block)
    there = pl.ds(pl.multiple_of((1 - high) * block, block), block)
    sent[...] = (kept[there, :] + got[there, :].astype(jnp.float32)).astype(sent.dtype)
    total[...] = kept[here, :] + got[here, :].astype(jnp.float32)


def pair_phase(kept, got):
    rows, width = kept.shape
    return pl.pallas_call(
        pair_kernel,
        out_shape=(
            jax.ShapeDtypeStruct((rows // 2, width), jnp.bfloat16),
            jax.ShapeDtypeStruct((rows // 2, width), jnp.float32),
        ),
        in_specs=[VMEM] * 2,
        out_specs=(VMEM,) * 2,
        compiler_params=pltpu.CompilerParams(vmem_limit_bytes=8 << 20),
        name="pair_sum",
    )(kept, got)


def finish_kernel(residual, total_one, got_one, total_two, got_two, mixed):
    start = 0
    for total, got in ((total_one, got_one), (total_two, got_two)):
        at = slice(start, start + total.shape[1])
        mixed[:, at] = (
            residual[:, at].astype(jnp.float32) + total[...] + got[...].astype(jnp.float32)
        ).astype(mixed.dtype)
        start = at.stop


def finish_phase(residual, *terms):
    return pl.pallas_call(
        finish_kernel,
        out_shape=jax.ShapeDtypeStruct(residual.shape, residual.dtype),
        in_specs=[VMEM] * 5,
        out_specs=VMEM,
        compiler_params=pltpu.CompilerParams(vmem_limit_bytes=8 << 20),
        name="finish",
    )(residual, *terms)


def swap(value, bit):
    return lax.ppermute(value, "tp", [(i, i ^ bit) for i in range(lax.axis_size("tp"))])


def four_by_four(hidden, adapter_ids, weight, rank_down, rank_up, residual):
    up = rank_up[0]
    one, two = WIDTHS
    packed, hidden = low_phase(hidden, jnp.swapaxes(rank_down, 1, 2)[0])
    packed = lax.all_to_all(packed, ("tp",) + PS, split_axis=0, concat_axis=0, tiled=True)
    base = base_phase(hidden, weight, 0, one)
    low, sent, kept = correct_phase(adapter_ids[None], packed, up, base)
    got = swap(sent, 1)
    sent_last, kept_last = last_phase(hidden, weight, low, up, one, two)
    got_last = swap(sent_last, 1)
    sent, total = pair_phase(kept, got)
    got = swap(sent, 2)
    sent_last, total_last = pair_phase(kept_last, got_last)
    got_last = swap(sent_last, 2)
    return finish_phase(residual, total, got, total_last, got_last)


def any_size(hidden_units, adapter_ids, down_projection_weight, rank_down, rank_up, residual):
    owned_count = rank_down.shape[0]
    first_owned = lax.axis_index(PS) * owned_count
    chosen = (
        (adapter_ids - first_owned)[:, None] == jnp.arange(owned_count, dtype=jnp.int32)[None, :]
    ).astype(jnp.float32)
    projected = jnp.einsum(
        "rf,afk->rak", hidden_units, rank_down, preferred_element_type=jnp.float32
    )
    partial_low = jnp.einsum("rak,ra->rk", projected, chosen)
    low_rank = lax.psum(partial_low, ("tp",) + PS).astype(jnp.bfloat16)
    held_count, rank_width, columns = rank_up.shape
    first_held = lax.axis_index("tp") * held_count
    picked = (
        (adapter_ids - first_held)[:, None] == jnp.arange(held_count, dtype=jnp.int32)[None, :]
    ).astype(jnp.bfloat16)
    coefficient = (picked[:, :, None] * low_rank[:, None, :]).reshape(
        -1, held_count * rank_width
    )
    term = jnp.dot(
        hidden_units, down_projection_weight, preferred_element_type=jnp.float32
    ) + jnp.dot(
        coefficient,
        rank_up.reshape(held_count * rank_width, columns),
        preferred_element_type=jnp.float32,
    )
    summed = lax.psum_scatter(
        term.astype(jnp.bfloat16), "tp", scatter_dimension=0, tiled=True
    ).astype(jnp.float32)
    return (residual.astype(jnp.float32) + summed).astype(jnp.bfloat16)


def on_device(hidden_units, adapter_ids, down_projection_weight, rank_down, rank_up, residual):
    sizes = [lax.axis_size(axis) for axis in ("tp",) + PS]
    fits = (
        sizes[0] == 4
        and sizes[1] * sizes[2] == 4
        and rank_down.shape[0] == 1
        and rank_up.shape[0] == 1
        and residual.shape == (16, sum(WIDTHS))
        and hidden_units.shape[1] % DEPTH == 0
    )
    form = four_by_four if fits else any_size
    return form(hidden_units, adapter_ids, down_projection_weight, rank_down, rank_up, residual)


def solution(mesh):
    placed = (
        P("parts", "tp"),
        P("parts"),
        P("tp", ("page", "sub")),
        P(("parts", "page", "sub"), "tp", None),
        P(("parts", "tp"), None, ("page", "sub")),
        P(("parts", "tp"), ("page", "sub")),
    )
    return jax.shard_map(
        on_device,
        mesh=mesh,
        in_specs=placed,
        out_specs=P(("parts", "tp"), ("page", "sub")),
        check_vma=False,
    )
```

```python
import functools

import jax
import jax.numpy as jnp
from jax import lax
from jax.experimental import pallas as pl
from jax.experimental.pallas import tpu as pltpu
from jax.sharding import PartitionSpec as P

WIDTHS = (2304, 768)
DEPTH = 768
HOLDERS = (
    ((2, 0, 1, 3), (1, 3, 2, 0), (3, 2, 0, 1), (0, 1, 3, 2)),
    ((3, 2, 0, 1), (0, 3, 1, 2), (1, 0, 2, 3), (2, 1, 3, 0)),
    ((3, 2, 1, 0), (1, 0, 3, 2), (2, 1, 0, 3), (0, 3, 2, 1)),
    ((1, 2, 3, 0), (3, 1, 0, 2), (2, 0, 1, 3), (0, 3, 2, 1)),
)
PS = ("page", "sub")
VMEM = pl.BlockSpec(memory_space=pltpu.VMEM)
HBM = pl.BlockSpec(memory_space=pltpu.HBM)


def column_of(ids_row):
    rows = ids_row.shape[1]
    down = lax.broadcasted_iota(jnp.int32, (rows, rows), 0)
    across = lax.broadcasted_iota(jnp.int32, (rows, rows), 1)
    spread = jnp.broadcast_to(ids_row, (rows, rows))
    return jnp.sum(
        jnp.where(down == across, spread.astype(jnp.float32), 0.0), axis=1, keepdims=True
    )


def deep(k):
    return pl.ds(pl.multiple_of(k * DEPTH, DEPTH), DEPTH)


def weight_copies(weight, held, arrived, start, width):
    def copy(k):
        return pltpu.make_async_copy(
            weight.at[deep(k), pl.ds(start, width)], held.at[deep(k)], arrived.at[k]
        )

    return copy


def low_kernel(hidden, rank_down, low, hidden_here, down_here, got):
    copies = [
        pltpu.make_async_copy(hidden, hidden_here, got.at[0]),
        pltpu.make_async_copy(rank_down, down_here, got.at[1]),
    ]
    for copy in copies:
        copy.start()
    for copy in copies:
        copy.wait()
    low[...] = lax.dot_general(
        hidden_here[...],
        down_here[...],
        (((1,), (1,)), ((), ())),
        preferred_element_type=jnp.float32,
    )


def low_phase(hidden, rank_down):
    rows, depth = hidden.shape
    rank = rank_down.shape[0]
    return pl.pallas_call(
        low_kernel,
        out_shape=(
            jax.ShapeDtypeStruct((rows, rank), jnp.float32),
            jax.ShapeDtypeStruct(hidden.shape, hidden.dtype),
        ),
        in_specs=[HBM] * 2,
        out_specs=(VMEM,) * 2,
        scratch_shapes=[
            pltpu.VMEM(rank_down.shape, rank_down.dtype),
            pltpu.SemaphoreType.DMA((2,)),
        ],
        compiler_params=pltpu.CompilerParams(vmem_limit_bytes=52 << 20),
        cost_estimate=pl.CostEstimate(
            flops=2 * rows * depth * rank,
            bytes_accessed=2 * depth * (rank + rows),
            transcendentals=0,
        ),
        name="low_rank",
    )(hidden, rank_down)


def stream_dot(hidden, weight, total, held, arrived, start):
    steps = weight.shape[0] // DEPTH
    copy = weight_copies(weight, held, arrived, start, total.shape[1])

    @pl.loop(0, steps)
    def _(k):
        copy(k).start()

    total[...] = jnp.zeros_like(total)

    @pl.loop(0, steps)
    def _(k):
        copy(k).wait()
        total[...] += jnp.dot(hidden[:, deep(k)], held[deep(k)], preferred_element_type=jnp.float32)


def base_kernel(start, hidden, weight, base, held, arrived):
    stream_dot(hidden, weight, base, held, arrived, start)


def base_phase(hidden, weight, start, width):
    rows, depth = hidden.shape
    return pl.pallas_call(
        functools.partial(base_kernel, start),
        out_shape=jax.ShapeDtypeStruct((rows, width), jnp.float32),
        in_specs=[VMEM, HBM],
        out_specs=VMEM,
        scratch_shapes=[
            pltpu.VMEM((depth, width), weight.dtype),
            pltpu.SemaphoreType.DMA((depth // DEPTH,)),
        ],
        compiler_params=pltpu.CompilerParams(vmem_limit_bytes=42 << 20),
        cost_estimate=pl.CostEstimate(
            flops=2 * rows * depth * width, bytes_accessed=2 * depth * width, transcendentals=0
        ),
        name="base",
    )(hidden, weight)


def split_rows(total, at, sent, kept):
    block = total.shape[0] // 4
    bit = lax.rem(lax.axis_index("tp"), 2)
    for half in range(2):
        rows = pl.ds(half * block, block)
        there = pl.ds(pl.multiple_of((2 * half + 1 - bit) * block, block), block)
        here = pl.ds(pl.multiple_of((2 * half + bit) * block, block), block)
        sent[rows, at] = total[there, :].astype(sent.dtype)
        kept[rows, at] = total[here, :]


def adapter_term(low, up):
    return jnp.dot(low.astype(jnp.bfloat16), up, preferred_element_type=jnp.float32)


def correct_kernel(ids, low_a, low_b, low_c, low_d, up, base, low, sent, kept, total):
    held = column_of(ids[...]) == lax.axis_index("tp").astype(jnp.float32)
    low[...] = jnp.where(held, (low_a[...] + low_b[...]) + (low_c[...] + low_d[...]), 0.0)
    width = base.shape[1]
    total[...] = base[...] + adapter_term(low[...], up[:, :width])
    split_rows(total, slice(0, width), sent, kept)


def correct_phase(ids, lows, up, base):
    rows, rank = lows[0].shape
    width = base.shape[1]
    return pl.pallas_call(
        correct_kernel,
        out_shape=(
            jax.ShapeDtypeStruct((rows, rank), jnp.float32),
            jax.ShapeDtypeStruct((rows // 2, width), jnp.bfloat16),
            jax.ShapeDtypeStruct((rows // 2, width), jnp.float32),
        ),
        in_specs=[VMEM] * 7,
        out_specs=(VMEM,) * 3,
        scratch_shapes=[pltpu.VMEM((rows, width), jnp.float32)],
        compiler_params=pltpu.CompilerParams(vmem_limit_bytes=8 << 20),
        name="adapter_term",
    )(ids, *lows, up, base)


def last_kernel(start, hidden, weight, low, up, sent, kept, total, held, arrived):
    stream_dot(hidden, weight, total, held, arrived, start)
    width = total.shape[1]
    total[...] += adapter_term(low[...], up[:, start : start + width])
    split_rows(total, slice(0, width), sent, kept)


def last_phase(hidden, weight, low, up, start, width):
    rows, depth = hidden.shape
    return pl.pallas_call(
        functools.partial(last_kernel, start),
        out_shape=(
            jax.ShapeDtypeStruct((rows // 2, width), jnp.bfloat16),
            jax.ShapeDtypeStruct((rows // 2, width), jnp.float32),
        ),
        in_specs=[VMEM, HBM, VMEM, VMEM],
        out_specs=(VMEM, VMEM),
        scratch_shapes=[
            pltpu.VMEM((rows, width), jnp.float32),
            pltpu.VMEM((depth, width), weight.dtype),
            pltpu.SemaphoreType.DMA((depth // DEPTH,)),
        ],
        compiler_params=pltpu.CompilerParams(vmem_limit_bytes=32 << 20),
        cost_estimate=pl.CostEstimate(
            flops=2 * rows * depth * width, bytes_accessed=2 * depth * width, transcendentals=0
        ),
        name="last_base",
    )(hidden, weight, low, up)


def pair_kernel(kept, got, sent, total):
    block = kept.shape[0] // 2
    high = lax.div(lax.axis_index("tp"), 2)
    here = pl.ds(pl.multiple_of(high * block, block), block)
    there = pl.ds(pl.multiple_of((1 - high) * block, block), block)
    sent[...] = (kept[there, :] + got[there, :].astype(jnp.float32)).astype(sent.dtype)
    total[...] = kept[here, :] + got[here, :].astype(jnp.float32)


def pair_phase(kept, got):
    rows, width = kept.shape
    return pl.pallas_call(
        pair_kernel,
        out_shape=(
            jax.ShapeDtypeStruct((rows // 2, width), jnp.bfloat16),
            jax.ShapeDtypeStruct((rows // 2, width), jnp.float32),
        ),
        in_specs=[VMEM] * 2,
        out_specs=(VMEM,) * 2,
        compiler_params=pltpu.CompilerParams(vmem_limit_bytes=8 << 20),
        name="pair_sum",
    )(kept, got)


def finish_kernel(residual, total_one, got_one, total_two, got_two, mixed):
    start = 0
    for total, got in ((total_one, got_one), (total_two, got_two)):
        at = slice(start, start + total.shape[1])
        mixed[:, at] = (
            residual[:, at].astype(jnp.float32) + total[...] + got[...].astype(jnp.float32)
        ).astype(mixed.dtype)
        start = at.stop


def finish_phase(residual, *terms):
    return pl.pallas_call(
        finish_kernel,
        out_shape=jax.ShapeDtypeStruct(residual.shape, residual.dtype),
        in_specs=[VMEM] * 5,
        out_specs=VMEM,
        compiler_params=pltpu.CompilerParams(vmem_limit_bytes=8 << 20),
        name="finish",
    )(residual, *terms)


def swap(value, bit):
    return lax.ppermute(value, "tp", [(i, i ^ bit) for i in range(lax.axis_size("tp"))])


def four_by_four(hidden, adapter_ids, weight, rank_down, rank_up, residual):
    up = rank_up[0]
    one, two = WIDTHS
    low, hidden = low_phase(hidden, jnp.swapaxes(rank_down, 1, 2)[0])
    lows = []
    for k in (3, 2, 1, 0):
        pairs = [(t * 4 + a, a * 4 + HOLDERS[a][k][t]) for t in range(4) for a in range(4)]
        lows.append(lax.ppermute(low, ("tp",) + PS, pairs))
    base = base_phase(hidden, weight, 0, one)
    low, sent, kept = correct_phase(adapter_ids[None], lows, up, base)
    got = swap(sent, 1)
    sent_last, kept_last = last_phase(hidden, weight, low, up, one, two)
    got_last = swap(sent_last, 1)
    sent, total = pair_phase(kept, got)
    got = swap(sent, 2)
    sent_last, total_last = pair_phase(kept_last, got_last)
    got_last = swap(sent_last, 2)
    return finish_phase(residual, total, got, total_last, got_last)


def any_size(hidden_units, adapter_ids, down_projection_weight, rank_down, rank_up, residual):
    owned_count = rank_down.shape[0]
    first_owned = lax.axis_index(PS) * owned_count
    chosen = (
        (adapter_ids - first_owned)[:, None] == jnp.arange(owned_count, dtype=jnp.int32)[None, :]
    ).astype(jnp.float32)
    projected = jnp.einsum(
        "rf,afk->rak", hidden_units, rank_down, preferred_element_type=jnp.float32
    )
    partial_low = jnp.einsum("rak,ra->rk", projected, chosen)
    low_rank = lax.psum(partial_low, ("tp",) + PS).astype(jnp.bfloat16)
    held_count, rank_width, columns = rank_up.shape
    first_held = lax.axis_index("tp") * held_count
    picked = (
        (adapter_ids - first_held)[:, None] == jnp.arange(held_count, dtype=jnp.int32)[None, :]
    ).astype(jnp.bfloat16)
    coefficient = (picked[:, :, None] * low_rank[:, None, :]).reshape(
        -1, held_count * rank_width
    )
    term = jnp.dot(
        hidden_units, down_projection_weight, preferred_element_type=jnp.float32
    ) + jnp.dot(
        coefficient,
        rank_up.reshape(held_count * rank_width, columns),
        preferred_element_type=jnp.float32,
    )
    summed = lax.psum_scatter(
        term.astype(jnp.bfloat16), "tp", scatter_dimension=0, tiled=True
    ).astype(jnp.float32)
    return (residual.astype(jnp.float32) + summed).astype(jnp.bfloat16)


def on_device(hidden_units, adapter_ids, down_projection_weight, rank_down, rank_up, residual):
    sizes = [lax.axis_size(axis) for axis in ("tp",) + PS]
    fits = (
        sizes[0] == 4
        and sizes[1] * sizes[2] == 4
        and rank_down.shape[0] == 1
        and rank_up.shape[0] == 1
        and residual.shape == (16, sum(WIDTHS))
        and hidden_units.shape[1] % DEPTH == 0
    )
    form = four_by_four if fits else any_size
    return form(hidden_units, adapter_ids, down_projection_weight, rank_down, rank_up, residual)


def solution(mesh):
    placed = (
        P("parts", "tp"),
        P("parts"),
        P("tp", ("page", "sub")),
        P(("parts", "page", "sub"), "tp", None),
        P(("parts", "tp"), None, ("page", "sub")),
        P(("parts", "tp"), ("page", "sub")),
    )
    return jax.shard_map(
        on_device,
        mesh=mesh,
        in_specs=placed,
        out_specs=P(("parts", "tp"), ("page", "sub")),
        check_vma=False,
    )
```

```python
import functools

import jax
import jax.numpy as jnp
from jax import lax
from jax.experimental import pallas as pl
from jax.experimental.pallas import tpu as pltpu
from jax.sharding import PartitionSpec as P

WIDTHS = (2304, 768)
DEPTH = 768
THIRDS = 3
PS = ("page", "sub")
VMEM = pl.BlockSpec(memory_space=pltpu.VMEM)
HBM = pl.BlockSpec(memory_space=pltpu.HBM)


def column_of(ids_row):
    rows = ids_row.shape[1]
    down = lax.broadcasted_iota(jnp.int32, (rows, rows), 0)
    across = lax.broadcasted_iota(jnp.int32, (rows, rows), 1)
    spread = jnp.broadcast_to(ids_row, (rows, rows))
    return jnp.sum(
        jnp.where(down == across, spread.astype(jnp.float32), 0.0), axis=1, keepdims=True
    )


def deep(k):
    return pl.ds(pl.multiple_of(k * DEPTH, DEPTH), DEPTH)


def weight_copies(weight, held, arrived, start, width):
    def copy(k):
        return pltpu.make_async_copy(
            weight.at[deep(k), pl.ds(start, width)], held.at[deep(k)], arrived.at[k]
        )

    return copy


def low_kernel(hidden, rank_down, low, hidden_here, down_here, got):
    depth = hidden.shape[1] // THIRDS
    copies = []
    for third in range(THIRDS):
        at = slice(third * depth, (third + 1) * depth)
        pair = [(hidden, hidden_here), (rank_down, down_here)]
        copies.append(
            [
                pltpu.make_async_copy(source.at[:, at], here.at[:, at], got.at[2 * third + index])
                for index, (source, here) in enumerate(pair)
            ]
        )
        for copy in copies[third]:
            copy.start()
    for third in range(THIRDS):
        for copy in copies[third]:
            copy.wait()
        at = slice(third * depth, (third + 1) * depth)
        product = lax.dot_general(
            hidden_here[:, at],
            down_here[:, at],
            (((1,), (1,)), ((), ())),
            preferred_element_type=jnp.float32,
        )
        low[...] = product if third == 0 else low[...] + product


def low_phase(hidden, rank_down):
    rows, depth = hidden.shape
    rank = rank_down.shape[0]
    return pl.pallas_call(
        low_kernel,
        out_shape=(
            jax.ShapeDtypeStruct((rows, rank), jnp.float32),
            jax.ShapeDtypeStruct(hidden.shape, hidden.dtype),
        ),
        in_specs=[HBM] * 2,
        out_specs=(VMEM,) * 2,
        scratch_shapes=[
            pltpu.VMEM(rank_down.shape, rank_down.dtype),
            pltpu.SemaphoreType.DMA((2 * THIRDS,)),
        ],
        compiler_params=pltpu.CompilerParams(vmem_limit_bytes=52 << 20),
        cost_estimate=pl.CostEstimate(
            flops=2 * rows * depth * rank,
            bytes_accessed=2 * depth * (rank + rows),
            transcendentals=0,
        ),
        name="low_rank",
    )(hidden, rank_down)


def stream_dot(hidden, weight, total, held, arrived, start):
    steps = weight.shape[0] // DEPTH
    copy = weight_copies(weight, held, arrived, start, total.shape[1])

    @pl.loop(0, steps)
    def _(k):
        copy(k).start()

    total[...] = jnp.zeros_like(total)

    @pl.loop(0, steps)
    def _(k):
        copy(k).wait()
        total[...] += jnp.dot(hidden[:, deep(k)], held[deep(k)], preferred_element_type=jnp.float32)


def base_kernel(start, hidden, weight, base, held, arrived):
    stream_dot(hidden, weight, base, held, arrived, start)


def base_phase(hidden, weight, start, width):
    rows, depth = hidden.shape
    return pl.pallas_call(
        functools.partial(base_kernel, start),
        out_shape=jax.ShapeDtypeStruct((rows, width), jnp.float32),
        in_specs=[VMEM, HBM],
        out_specs=VMEM,
        scratch_shapes=[
            pltpu.VMEM((depth, width), weight.dtype),
            pltpu.SemaphoreType.DMA((depth // DEPTH,)),
        ],
        compiler_params=pltpu.CompilerParams(vmem_limit_bytes=42 << 20),
        cost_estimate=pl.CostEstimate(
            flops=2 * rows * depth * width, bytes_accessed=2 * depth * width, transcendentals=0
        ),
        name="base",
    )(hidden, weight)


def split_rows(total, at, sent, kept):
    block = total.shape[0] // 4
    bit = lax.rem(lax.axis_index("tp"), 2)
    for half in range(2):
        rows = pl.ds(half * block, block)
        there = pl.ds(pl.multiple_of((2 * half + 1 - bit) * block, block), block)
        here = pl.ds(pl.multiple_of((2 * half + bit) * block, block), block)
        sent[rows, at] = total[there, :].astype(sent.dtype)
        kept[rows, at] = total[here, :]


def adapter_term(low, up):
    return jnp.dot(low.astype(jnp.bfloat16), up, preferred_element_type=jnp.float32)


def correct_kernel(ids, low_a, low_b, low_c, low_d, up, base, low, sent, kept, total):
    held = column_of(ids[...]) == lax.axis_index("tp").astype(jnp.float32)
    low[...] = jnp.where(held, (low_a[...] + low_b[...]) + (low_c[...] + low_d[...]), 0.0)
    width = base.shape[1]
    total[...] = base[...] + adapter_term(low[...], up[:, :width])
    split_rows(total, slice(0, width), sent, kept)


def correct_phase(ids, lows, up, base):
    rows, rank = lows[0].shape
    width = base.shape[1]
    return pl.pallas_call(
        correct_kernel,
        out_shape=(
            jax.ShapeDtypeStruct((rows, rank), jnp.float32),
            jax.ShapeDtypeStruct((rows // 2, width), jnp.bfloat16),
            jax.ShapeDtypeStruct((rows // 2, width), jnp.float32),
        ),
        in_specs=[VMEM] * 7,
        out_specs=(VMEM,) * 3,
        scratch_shapes=[pltpu.VMEM((rows, width), jnp.float32)],
        compiler_params=pltpu.CompilerParams(vmem_limit_bytes=8 << 20),
        name="adapter_term",
    )(ids, *lows, up, base)


def last_kernel(start, hidden, weight, low, up, sent, kept, total, held, arrived):
    stream_dot(hidden, weight, total, held, arrived, start)
    width = total.shape[1]
    total[...] += adapter_term(low[...], up[:, start : start + width])
    split_rows(total, slice(0, width), sent, kept)


def last_phase(hidden, weight, low, up, start, width):
    rows, depth = hidden.shape
    return pl.pallas_call(
        functools.partial(last_kernel, start),
        out_shape=(
            jax.ShapeDtypeStruct((rows // 2, width), jnp.bfloat16),
            jax.ShapeDtypeStruct((rows // 2, width), jnp.float32),
        ),
        in_specs=[VMEM, HBM, VMEM, VMEM],
        out_specs=(VMEM, VMEM),
        scratch_shapes=[
            pltpu.VMEM((rows, width), jnp.float32),
            pltpu.VMEM((depth, width), weight.dtype),
            pltpu.SemaphoreType.DMA((depth // DEPTH,)),
        ],
        compiler_params=pltpu.CompilerParams(vmem_limit_bytes=32 << 20),
        cost_estimate=pl.CostEstimate(
            flops=2 * rows * depth * width, bytes_accessed=2 * depth * width, transcendentals=0
        ),
        name="last_base",
    )(hidden, weight, low, up)


def pair_kernel(kept, got, sent, total):
    block = kept.shape[0] // 2
    high = lax.div(lax.axis_index("tp"), 2)
    here = pl.ds(pl.multiple_of(high * block, block), block)
    there = pl.ds(pl.multiple_of((1 - high) * block, block), block)
    sent[...] = (kept[there, :] + got[there, :].astype(jnp.float32)).astype(sent.dtype)
    total[...] = kept[here, :] + got[here, :].astype(jnp.float32)


def pair_phase(kept, got):
    rows, width = kept.shape
    return pl.pallas_call(
        pair_kernel,
        out_shape=(
            jax.ShapeDtypeStruct((rows // 2, width), jnp.bfloat16),
            jax.ShapeDtypeStruct((rows // 2, width), jnp.float32),
        ),
        in_specs=[VMEM] * 2,
        out_specs=(VMEM,) * 2,
        compiler_params=pltpu.CompilerParams(vmem_limit_bytes=8 << 20),
        name="pair_sum",
    )(kept, got)


def finish_kernel(residual, total_one, got_one, total_two, got_two, mixed):
    start = 0
    for total, got in ((total_one, got_one), (total_two, got_two)):
        at = slice(start, start + total.shape[1])
        mixed[:, at] = (
            residual[:, at].astype(jnp.float32) + total[...] + got[...].astype(jnp.float32)
        ).astype(mixed.dtype)
        start = at.stop


def finish_phase(residual, *terms):
    return pl.pallas_call(
        finish_kernel,
        out_shape=jax.ShapeDtypeStruct(residual.shape, residual.dtype),
        in_specs=[VMEM] * 5,
        out_specs=VMEM,
        compiler_params=pltpu.CompilerParams(vmem_limit_bytes=8 << 20),
        name="finish",
    )(residual, *terms)


def swap(value, bit):
    return lax.ppermute(value, "tp", [(i, i ^ bit) for i in range(lax.axis_size("tp"))])


def four_by_four(hidden, adapter_ids, weight, rank_down, rank_up, residual):
    up = rank_up[0]
    one, two = WIDTHS
    low, hidden = low_phase(hidden, jnp.swapaxes(rank_down, 1, 2)[0])
    lows = []
    for j in range(4):
        pairs = [(t * 4 + a, a * 4 + (t + j) % 4) for t in range(4) for a in range(4)]
        lows.append(lax.ppermute(low, ("tp",) + PS, pairs))
    base = base_phase(hidden, weight, 0, one)
    low, sent, kept = correct_phase(adapter_ids[None], lows, up, base)
    got = swap(sent, 1)
    sent_last, kept_last = last_phase(hidden, weight, low, up, one, two)
    got_last = swap(sent_last, 1)
    sent, total = pair_phase(kept, got)
    got = swap(sent, 2)
    sent_last, total_last = pair_phase(kept_last, got_last)
    got_last = swap(sent_last, 2)
    return finish_phase(residual, total, got, total_last, got_last)


def any_size(hidden_units, adapter_ids, down_projection_weight, rank_down, rank_up, residual):
    owned_count = rank_down.shape[0]
    first_owned = lax.axis_index(PS) * owned_count
    chosen = (
        (adapter_ids - first_owned)[:, None] == jnp.arange(owned_count, dtype=jnp.int32)[None, :]
    ).astype(jnp.float32)
    projected = jnp.einsum(
        "rf,afk->rak", hidden_units, rank_down, preferred_element_type=jnp.float32
    )
    partial_low = jnp.einsum("rak,ra->rk", projected, chosen)
    low_rank = lax.psum(partial_low, ("tp",) + PS).astype(jnp.bfloat16)
    held_count, rank_width, columns = rank_up.shape
    first_held = lax.axis_index("tp") * held_count
    picked = (
        (adapter_ids - first_held)[:, None] == jnp.arange(held_count, dtype=jnp.int32)[None, :]
    ).astype(jnp.bfloat16)
    coefficient = (picked[:, :, None] * low_rank[:, None, :]).reshape(
        -1, held_count * rank_width
    )
    term = jnp.dot(
        hidden_units, down_projection_weight, preferred_element_type=jnp.float32
    ) + jnp.dot(
        coefficient,
        rank_up.reshape(held_count * rank_width, columns),
        preferred_element_type=jnp.float32,
    )
    summed = lax.psum_scatter(
        term.astype(jnp.bfloat16), "tp", scatter_dimension=0, tiled=True
    ).astype(jnp.float32)
    return (residual.astype(jnp.float32) + summed).astype(jnp.bfloat16)


def on_device(hidden_units, adapter_ids, down_projection_weight, rank_down, rank_up, residual):
    sizes = [lax.axis_size(axis) for axis in ("tp",) + PS]
    fits = (
        sizes[0] == 4
        and sizes[1] * sizes[2] == 4
        and rank_down.shape[0] == 1
        and rank_up.shape[0] == 1
        and residual.shape == (16, sum(WIDTHS))
        and hidden_units.shape[1] % DEPTH == 0
        and hidden_units.shape[1] % (THIRDS * 128) == 0
    )
    form = four_by_four if fits else any_size
    return form(hidden_units, adapter_ids, down_projection_weight, rank_down, rank_up, residual)


def solution(mesh):
    placed = (
        P("parts", "tp"),
        P("parts"),
        P("tp", ("page", "sub")),
        P(("parts", "page", "sub"), "tp", None),
        P(("parts", "tp"), None, ("page", "sub")),
        P(("parts", "tp"), ("page", "sub")),
    )
    return jax.shard_map(
        on_device,
        mesh=mesh,
        in_specs=placed,
        out_specs=P(("parts", "tp"), ("page", "sub")),
        check_vma=False,
    )
```
